32 devices in a mesh: node: 4 (over y, x), grid: 8 (over z, core).
Axes of the slice: x: 2, y: 2, z: 4, core: 2. Of those that a mesh axis runs over, the one named last changes fastest.
Arguments:
- probes: float32 [1, 48, 192, 256], P(None, 'grid'), may hold values from -6 to 6
- potential: float32 [48, 192, 256], P('grid'), may hold values from -2 to 1
- warm_start: bfloat16 [4, 1, 2, 48, 192, 256], P('node', None, None, 'grid'), may hold values from -0.29882812 to 0.29882812
- shift_points: float32 [4, 2], P('node'), may hold values from -4 to 9, as said below
- quad_weights: float32 [4, 2], P('node'), may hold values from -0.3 to 0.3
Outputs:
- moments: float32 [2, 1, 2, 48, 192, 256], P(None, None, None, 'grid', 'node')
- trace_estimate: float32 [2], replicated
The draws below stay inside these ranges and needn't reach their ends.
Inputs may be any that keep to these rules, and one draw needn't show every extreme that they name: `shift_points`: column 0 holds real parts in -1 to 9; column 1 holds imaginary parts whose magnitude lies in 1 to 4.
All inputs are finite; a program needn't handle non-finite values.
Results may differ from the reference program's by a relative error of at most 0.0003.
Values may be sent and summed in bfloat16 or wider, within the bound.
A program may use at most 192 MiB of HBM per device.

```python
import math
import jax
import jax.numpy as jnp
from jax import lax

NX = 192
NY = 256
PROBES = 1
ITERS = 2
MOMENTS = 2
NZ = 48
SHIFTS = 4


def draw_shift_points(key, part):
    key_real, key_size, key_sign = jax.random.split(key, 3)
    real_part = jax.random.uniform(key_real, (SHIFTS,), jnp.float32, -1.0, 9.0)
    magnitude = jnp.exp(jax.random.uniform(key_size, (SHIFTS,), jnp.float32, 0.0, math.log(4.0)))
    signs = jnp.where(jax.random.bernoulli(key_sign, 0.5, (SHIFTS,)), 1.0, -1.0).astype(jnp.float32)
    return jnp.stack([real_part, signs * magnitude], axis=1)


def levels(stream_key, dims, pieces, low, largest):
    level, own = 1.0, jax.random.fold_in(stream_key, 6)
    for axis_at, blocks in pieces:
        heights = jnp.exp(jax.random.uniform(jax.random.fold_in(own, axis_at), (blocks,), jnp.float32, low / len(pieces), largest / len(pieces)))
        level = level * jnp.repeat(heights, dims[axis_at] // blocks).reshape([-1 if axis == axis_at else 1 for axis in range(len(dims))])
    return level


def bell_draw(key, shape, deviation, most, pieces=(), held_as=jnp.bfloat16):
    result = deviation * jax.random.normal(key, shape, jnp.float32)
    if pieces:
        result = result * levels(key, shape, pieces, -0.22, 0.18)
    return jnp.clip(result, -most, most).astype(held_as)


def setup_inputs(seed: int = 0) -> dict:
    key_of = jax.random.split(jax.random.key(seed), 6)
    return {
        "probes": bell_draw(key_of[0], (PROBES, NZ, NX, NY), 1.0, 6.0, ((1, 8),), jnp.float32),
        "potential": jnp.clip(-2.0 + 3.0 * jax.random.uniform(key_of[1], (NZ, NX, NY), jnp.float32) ** levels(key_of[1], (NZ, NX, NY), ((0, 8),), -0.2, 0.2), -2.0, 1.0),
        "warm_start": bell_draw(key_of[2], (SHIFTS, PROBES, 2, NZ, NX, NY), 0.05, 0.29882812, ((0, 4), (3, 8))),
        "shift_points": draw_shift_points(jax.random.fold_in(key_of[5], 71), 0),
        "quad_weights": jnp.clip(jax.random.uniform(key_of[4], (SHIFTS, 2), jnp.float32, -0.3, 0.3) * levels(key_of[4], (SHIFTS, 2), ((0, 4),), -0.4, 0.0), -0.3, 0.3),
    }


near_weight = 4.0 / 3.0
far_weight = -1.0 / 12.0
self_weight = -7.5


def hamiltonian_apply(padded, potential, shift_real, shift_imag):
    middle = padded[:, :, :, 2:-2]
    near_sum = (padded[:, :, :, 1:-3] + padded[:, :, :, 3:-1]) + (jnp.roll(middle, 1, 4) + jnp.roll(middle, -1, 4)) + (jnp.roll(middle, 1, 5) + jnp.roll(middle, -1, 5))
    far_sum = (padded[:, :, :, :-4] + padded[:, :, :, 4:]) + (jnp.roll(middle, 2, 4) + jnp.roll(middle, -2, 4)) + (jnp.roll(middle, 2, 5) + jnp.roll(middle, -2, 5))
    laplacian = near_weight * near_sum + far_weight * far_sum + self_weight * middle
    real_shift = shift_real[:, None, None, None, None]
    imag_shift = shift_imag[:, None, None, None, None]
    real_part = middle[:, :, 0]
    imag_part = middle[:, :, 1]
    result_real = real_shift * real_part - imag_shift * imag_part + 0.5 * laplacian[:, :, 0] - potential * real_part
    result_imag = real_shift * imag_part + imag_shift * real_part + 0.5 * laplacian[:, :, 1] - potential * imag_part
    return jnp.stack([result_real, result_imag], axis=2)


def wrap_pad(vector):
    return jnp.concatenate([vector[:, :, :, -2:], vector, vector[:, :, :, :2]], axis=3)


def bilinear(first_vec, second_vec):
    real_sum = jnp.sum(first_vec[:, :, 0] * second_vec[:, :, 0] - first_vec[:, :, 1] * second_vec[:, :, 1], axis=(2, 3, 4))
    imag_sum = jnp.sum(first_vec[:, :, 0] * second_vec[:, :, 1] + first_vec[:, :, 1] * second_vec[:, :, 0], axis=(2, 3, 4))
    return jnp.stack([real_sum, imag_sum], axis=-1)


def complex_times(factor_one, factor_two):
    return jnp.stack([factor_one[..., 0] * factor_two[..., 0] - factor_one[..., 1] * factor_two[..., 1], factor_one[..., 0] * factor_two[..., 1] + factor_one[..., 1] * factor_two[..., 0]], axis=-1)


def complex_divide(factor_one, factor_two):
    magnitude = factor_two[..., 0] * factor_two[..., 0] + factor_two[..., 1] * factor_two[..., 1]
    return jnp.stack([(factor_one[..., 0] * factor_two[..., 0] + factor_one[..., 1] * factor_two[..., 1]) / magnitude, (factor_one[..., 1] * factor_two[..., 0] - factor_one[..., 0] * factor_two[..., 1]) / magnitude], axis=-1)


def scale_field(scalars, vector):
    real_scalar = scalars[..., 0][:, :, None, None, None]
    imag_scalar = scalars[..., 1][:, :, None, None, None]
    return jnp.stack([real_scalar * vector[:, :, 0] - imag_scalar * vector[:, :, 1], real_scalar * vector[:, :, 1] + imag_scalar * vector[:, :, 0]], axis=2)


def cocg_shift(start_guess, source, potential, shift_real, shift_imag):
    solution = start_guess
    residual = source - hamiltonian_apply(wrap_pad(start_guess), potential, shift_real, shift_imag)
    direction = residual
    norm_now = bilinear(residual, residual)
    for iteration in range(ITERS):
        applied = hamiltonian_apply(wrap_pad(direction), potential, shift_real, shift_imag)
        step_length = complex_divide(norm_now, bilinear(direction, applied))
        solution = solution + scale_field(step_length, direction)
        residual = residual - scale_field(step_length, applied)
        if iteration + 1 < ITERS:
            norm_next = bilinear(residual, residual)
            direction = residual + scale_field(complex_divide(norm_next, norm_now), direction)
            norm_now = norm_next
    return solution


def reference(probes, potential, warm_start, shift_points, quad_weights):
    source = jnp.stack([probes, jnp.zeros_like(probes)], axis=1)[None]

    def shift_step(running, inputs):
        moments, trace_value = running
        start_guess, shift_point, weight = inputs
        solution = cocg_shift(start_guess.astype(jnp.float32)[None], source, potential, shift_point[0:1], shift_point[1:2])[0]
        scaled_shift = jnp.stack([(shift_point[0] - 4.0) / 5.0, shift_point[1] / 5.0])
        weight_power = weight
        moment_terms = []
        for degree in range(MOMENTS):
            moment_terms.append(jnp.stack([weight_power[0] * solution[:, 0] - weight_power[1] * solution[:, 1], weight_power[0] * solution[:, 1] + weight_power[1] * solution[:, 0]], axis=1))
            weight_power = complex_times(weight_power, scaled_shift)
        moments = moments + jnp.stack(moment_terms)
        inner_sum = jnp.stack([jnp.sum(probes * solution[:, 0]), jnp.sum(probes * solution[:, 1])]) / PROBES
        trace_value = trace_value + complex_times(weight, inner_sum)
        return (moments, trace_value), None

    initial = (jnp.zeros((MOMENTS, PROBES, 2, NZ, NX, NY), jnp.float32), jnp.zeros((2,), jnp.float32))
    (moments, trace_value), unused_out = lax.scan(shift_step, initial, (warm_start, shift_points, quad_weights))
    return moments, trace_value
```

```python
import functools

import jax
import jax.numpy as jnp
import ml_dtypes
import numpy as np
from jax import lax
from jax.experimental import pallas as pl
from jax.experimental.pallas import tpu as pltpu
from jax.sharding import PartitionSpec as P

MESH = pl.DeviceIdType.MESH
SUMS = 16
CHUNK = 32


def ring_matrix(size, diagonal):
    matrix = np.zeros((size, size), np.float32)
    at = np.arange(size)
    for step, weight in ((1, 16.0), (2, -1.0)):
        matrix[at, (at + step) % size] += weight
        matrix[at, (at - step) % size] += weight
    matrix[at, at] += diagonal
    return matrix.astype(ml_dtypes.bfloat16)


def cmul(a, b):
    return a[0] * b[0] - a[1] * b[1], a[0] * b[1] + a[1] * b[0]


def cdiv(a, b):
    size = b[0] * b[0] + b[1] * b[1]
    return (a[0] * b[0] + a[1] * b[1]) / size, (a[1] * b[0] - a[0] * b[1]) / size


def fold(values):
    rows, cols = values.shape
    return jnp.sum(values.reshape(rows // 8, 8, cols), axis=0)


def kernel(
    nodes,
    slabs,
    warm,
    probes,
    potential,
    shift_ref,
    weight_ref,
    along_x,
    along_y,
    moments,
    trace,
    xbuf,
    bbuf,
    vbuf,
    rbuf,
    qbuf,
    qlow,
    plane,
    acc,
    sums,
    final,
    arrived,
    notes,
    local_sem,
    x_send,
    x_recv,
    r_send,
    r_recv,
    q_send,
    q_recv,
    s_send,
    s_recv,
    n_send,
    n_recv,
    f_send,
    f_recv,
):
    node, slab = lax.axis_index("node"), lax.axis_index("grid")
    depth, width, length = bbuf.shape
    half = width // 2
    block = width // nodes
    above = (node, lax.rem(slab + 1, slabs))
    below = (node, lax.rem(slab + slabs - 1, slabs))

    loads = [
        pltpu.make_async_copy(warm.at[0, 0], xbuf.at[:, 2 : depth + 2], local_sem.at[0]),
        pltpu.make_async_copy(probes.at[0], bbuf, local_sem.at[1]),
        pltpu.make_async_copy(potential, vbuf, local_sem.at[2]),
    ]
    for load in loads:
        load.start()

    barrier = pltpu.get_barrier_semaphore()
    for k in range(1, slabs):
        pl.semaphore_signal(
            barrier, inc=1, device_id=(node, lax.rem(slab + k, slabs)), device_id_type=MESH
        )
    for k in range(1, nodes):
        pl.semaphore_signal(
            barrier, inc=1, device_id=(lax.rem(node + k, nodes), slab), device_id_type=MESH
        )
    pl.semaphore_wait(barrier, slabs + nodes - 2)

    def send(source, target, send_sem, recv_sem, device):
        copy = pltpu.make_async_remote_copy(
            src_ref=source,
            dst_ref=target,
            send_sem=send_sem,
            recv_sem=recv_sem,
            device_id=device,
            device_id_type=MESH,
        )
        copy.start()
        return copy

    x_down = send(
        warm.at[0, 0, :, 0:2], xbuf.at[:, depth + 2 : depth + 4], x_send.at[0], x_recv.at[0], below
    )
    x_up = send(warm.at[0, 0, :, depth - 2 : depth], xbuf.at[:, 0:2], x_send.at[1], x_recv.at[1], above)

    acc[...] = jnp.zeros_like(acc)
    qbuf[:, depth : depth + 2, half:, :] = jnp.zeros((2, 2, width - half, length), jnp.float32)
    shift = shift_ref[0, 0], shift_ref[0, 1]
    for load in loads:
        load.wait()

    def dot(a, b):
        return jnp.dot(a, b, preferred_element_type=jnp.float32)

    def in_plane_exact(p):
        for part in range(2):
            field = xbuf[part, p + 2]
            plane[part] = dot(field, along_y[...]) + dot(along_x[...], field)

    def in_plane(source, p):
        for part in range(2):
            field = source[part, p]
            high = field.astype(jnp.bfloat16)
            low = (field - high.astype(jnp.float32)).astype(jnp.bfloat16)
            plane[part] = (dot(high, along_y[...]) + dot(low, along_y[...])) + (
                dot(along_x[...], high) + dot(along_x[...], low)
            )

    def apply(field, stencil, local):
        diagonal = shift[0] - local
        return (
            diagonal * field[0] - shift[1] * field[1] + stencil[0] * (1.0 / 24.0),
            diagonal * field[1] + shift[1] * field[0] + stencil[1] * (1.0 / 24.0),
        )

    def in_chunks(first, terms):
        count = terms[1]

        def step(i, totals):
            rows = pl.ds(pl.multiple_of(i * CHUNK, CHUNK), CHUNK)
            values = terms[0](rows)
            return tuple(total + fold(value) for total, value in zip(totals, values))

        zero = jnp.zeros((8, length), jnp.float32)
        totals = lax.fori_loop(0, width // CHUNK, step, (zero,) * count)
        for i, total in enumerate(totals):
            acc[first + i] += total

    def residual_plane(p, carry):
        in_plane_exact(p)

        def terms(rows):
            stencil, field = [], []
            for part in range(2):
                at = [xbuf[part, p + j, rows, :].astype(jnp.float32) for j in range(5)]
                stencil.append(plane[part, rows, :] + 16.0 * (at[1] + at[3]) - (at[0] + at[4]))
                field.append(at[2])
            source = bbuf[p, rows, :]
            image = apply(field, stencil, vbuf[p, rows, :])
            r = source - image[0], -image[1]
            rbuf[0, p + 2, rows, :] = r[0]
            rbuf[1, p + 2, rows, :] = r[1]
            return (
                r[0] * r[0] - r[1] * r[1],
                2.0 * r[0] * r[1],
                source * field[0],
                source * field[1],
                source * r[0],
                source * r[1],
            )

        in_chunks(0, (terms, 6))
        return carry

    def image_plane(p, carry):
        in_plane(rbuf, p + 2)

        def terms(rows):
            stencil, field = [], []
            for part in range(2):
                at = [rbuf[part, p + j, rows, :] for j in range(5)]
                stencil.append(plane[part, rows, :] + 16.0 * (at[1] + at[3]) - (at[0] + at[4]))
                field.append(at[2])
            source = bbuf[p, rows, :]
            q = apply(field, stencil, vbuf[p, rows, :])
            qbuf[0, p, rows, :] = q[0]
            qbuf[1, p, rows, :] = q[1]
            return (
                *cmul(field, q),
                q[0] * q[0] - q[1] * q[1],
                2.0 * q[0] * q[1],
                source * q[0],
                source * q[1],
            )

        in_chunks(6, (terms, 6))
        return carry

    def energy_plane(p, carry):
        in_plane(qbuf, p)

        def terms(rows):
            stencil, field = [], []
            for part in range(2):
                stencil.append(
                    plane[part, rows, :]
                    + 32.0 * qbuf[part, p + 1, rows, :]
                    - 2.0 * qbuf[part, p + 2, rows, :]
                )
                field.append(qbuf[part, p, rows, :])
            return cmul(field, apply(field, stencil, vbuf[p, rows, :]))

        in_chunks(12, (terms, 2))
        return carry

    with jax.named_scope("residual"):
        lax.fori_loop(2, depth - 2, residual_plane, 0)
        x_up.wait_recv()
        x_down.wait_recv()
        lax.fori_loop(0, 2, residual_plane, 0)
        r_down = send(
            rbuf.at[:, 2:4], rbuf.at[:, depth + 2 : depth + 4], r_send.at[0], r_recv.at[0], below
        )
        lax.fori_loop(depth - 2, depth, residual_plane, 0)
        r_up = send(rbuf.at[:, depth : depth + 2], rbuf.at[:, 0:2], r_send.at[1], r_recv.at[1], above)

    with jax.named_scope("image"):
        lax.fori_loop(2, depth - 2, image_plane, 0)
        r_up.wait_recv()
        lax.fori_loop(0, 2, image_plane, 0)
        q_down = send(
            qbuf.at[:, 0:2, 0:half],
            qbuf.at[:, depth : depth + 2, 0:half],
            q_send.at[0],
            q_recv.at[0],
            below,
        )
        r_down.wait_recv()
        lax.fori_loop(depth - 2, depth, image_plane, 0)
        q_up = send(qbuf.at[:, depth - 2 : depth, half:width], qlow, q_send.at[1], q_recv.at[1], above)

    with jax.named_scope("energy"):
        lax.fori_loop(0, depth - 2, energy_plane, 0)
        q_down.wait_recv()
        lax.fori_loop(depth - 2, depth, energy_plane, 0)
        q_up.wait_recv()

        def crossing(i, totals):
            start = i * CHUNK
            mine = pl.ds(pl.multiple_of(half + start, CHUNK), CHUNK)
            theirs = pl.ds(pl.multiple_of(start, CHUNK), CHUNK)
            near = [qlow[part, 1, theirs, :] for part in range(2)]
            far = [qlow[part, 0, theirs, :] for part in range(2)]
            zeroth = [qbuf[part, 0, mine, :] for part in range(2)]
            first = [qbuf[part, 1, mine, :] for part in range(2)]
            one = cmul(zeroth, [32.0 * near[part] - 2.0 * far[part] for part in range(2)])
            two = cmul(first, near)
            return tuple(
                totals[part] + fold((one[part] - 2.0 * two[part]) * (1.0 / 24.0)) for part in range(2)
            )

        zero = jnp.zeros((8, length), jnp.float32)
        totals = lax.fori_loop(0, half // CHUNK, crossing, (zero, zero))
        acc[12] += totals[0]
        acc[13] += totals[1]

    with jax.named_scope("scalars"):
        partial = jnp.sum(acc[...], axis=1)
        lanes = partial[:, 0:128]
        for at in range(128, length, 128):
            lanes = lanes + partial[:, at : at + 128]
        sums[0] = lanes
        scalar_copies = [
            send(
                sums.at[0],
                sums.at[k],
                s_send.at[k],
                s_recv.at[k],
                (node, lax.rem(slab + k, slabs)),
            )
            for k in range(1, slabs)
        ]
        for copy in scalar_copies:
            copy.wait_recv()
        total = jnp.zeros((SUMS, 128), jnp.float32)
        for owner in range(slabs):
            total = total + sums[lax.rem(slab - owner + slabs, slabs)]
        total = jnp.broadcast_to(jnp.sum(total, axis=1, keepdims=True), (SUMS, length))
        pair = lambda i: (total[i : i + 1], total[i + 1 : i + 2])
        s0, t0, t1, s1, s2, t2, s3 = (pair(i) for i in range(0, 14, 2))
        step0 = cdiv(s0, s1)
        square = cmul(step0, step0)
        norm1 = cmul(square, s2)
        norm1 = norm1[0] - s0[0], norm1[1] - s0[1]
        ratio = cdiv(norm1, s0)
        grow = ratio[0] + 1.0, ratio[1]
        one = cmul(cmul(grow, grow), s1)
        two = cmul(cmul(grow, step0), s2)
        three = cmul(square, s3)
        step1 = cdiv(
            norm1, (one[0] - 2.0 * two[0] + three[0], one[1] - 2.0 * two[1] + three[1])
        )
        coef_r = cmul(step1, grow)
        coef_r = coef_r[0] + step0[0], coef_r[1] + step0[1]
        coef_q = cmul(step1, step0)
        coef_q = -coef_q[0], -coef_q[1]
        inner_r, inner_q = cmul(coef_r, t1), cmul(coef_q, t2)
        inner = t0[0] + inner_r[0] + inner_q[0], t0[1] + inner_r[1] + inner_q[1]
        weight = weight_ref[0, 0], weight_ref[0, 1]
        share = cmul(weight, inner)
        following = cmul(weight, ((shift[0] - 4.0) * 0.2, shift[1] * 0.2))
        row = lax.broadcasted_iota(jnp.int32, (8, 128), 0)
        note = jnp.zeros((8, 128), jnp.float32)
        entries = (*weight, *following, share[0][:, 0:128], share[1][:, 0:128])
        for i, entry in enumerate(entries):
            note = jnp.where(row == i, entry, note)
        notes[0] = note
        note_copies = [
            send(notes.at[0], notes.at[k], n_send.at[k], n_recv.at[k], (lax.rem(node + k, nodes), slab))
            for k in range(1, nodes)
        ]

    with jax.named_scope("solution_planes"):

        def final_plane(p, carry):
            def step(i, inner_carry):
                rows = pl.ds(pl.multiple_of(i * CHUNK, CHUNK), CHUNK)
                r = rbuf[0, p + 2, rows, :], rbuf[1, p + 2, rows, :]
                q = qbuf[0, p, rows, :], qbuf[1, p, rows, :]
                along_r, along_q = cmul(coef_r, r), cmul(coef_q, q)
                for part in range(2):
                    start = xbuf[part, p + 2, rows, :].astype(jnp.float32)
                    final[p, part, rows, :] = start + along_r[part] + along_q[part]
                return inner_carry

            lax.fori_loop(0, width // CHUNK, step, 0)
            return carry

        final_copies = []
        for p in range(depth):
            final_plane(p, 0)
            for k in range(1, nodes):
                peer = lax.rem(node + k, nodes)
                rows = pl.ds(pl.multiple_of(peer * block, 8), block)
                final_copies.append(
                    send(
                        final.at[p, :, rows, :],
                        arrived.at[k, p],
                        f_send.at[k, p],
                        f_recv.at[k, p],
                        (peer, slab),
                    )
                )

    with jax.named_scope("moments"):
        for copy in note_copies:
            copy.wait_recv()
        whole_trace = jnp.zeros((8, 128), jnp.float32)
        for owner in range(nodes):
            whole_trace = whole_trace + notes[lax.rem(node - owner + nodes, nodes)]
        lane = lax.broadcasted_iota(jnp.int32, (8, 128), 1)
        for part in range(2):
            trace[part] = jnp.sum(jnp.where((row == 4 + part) & (lane == 0), whole_trace, 0.0))
        weights = []
        for k in range(nodes):
            wide = jnp.broadcast_to(jnp.sum(jnp.where(lane == 0, notes[k], 0.0), axis=1, keepdims=True), (8, length))
            weights.append([(wide[i : i + 1], wide[i + 1 : i + 2]) for i in (0, 2)])
        own = pl.ds(pl.multiple_of(node * block, 8), block)
        for p in range(depth):
            for copy in final_copies[p * (nodes - 1) : (p + 1) * (nodes - 1)]:
                copy.wait_recv()
            fields = [(final[p, 0, own, :], final[p, 1, own, :])]
            for k in range(1, nodes):
                fields.append((arrived[k, p, 0], arrived[k, p, 1]))
            for degree in range(2):
                terms = [cmul(weights[k][degree], fields[k]) for k in range(nodes)]
                for part in range(2):
                    value = terms[0][part]
                    for term in terms[1:]:
                        value = value + term[part]
                    moments[degree, 0, part, p] = value

    for copy in [x_down, x_up, r_down, r_up, q_down, q_up, *scalar_copies, *note_copies, *final_copies]:
        copy.wait_send()


def per_device(nodes, slabs, probes, potential, warm_start, shift_points, quad_weights):
    depth, width, length = potential.shape
    block = width // nodes
    f32, bf16 = jnp.float32, jnp.bfloat16
    anywhere = pl.BlockSpec(memory_space=pl.ANY)
    scalars = pl.BlockSpec(memory_space=pltpu.SMEM)
    vector = pl.BlockSpec(memory_space=pltpu.VMEM)
    dma = pltpu.SemaphoreType.DMA
    return pl.pallas_call(
        functools.partial(kernel, nodes, slabs),
        out_shape=(
            jax.ShapeDtypeStruct((2, 1, 2, depth, block, length), f32),
            jax.ShapeDtypeStruct((2,), f32),
        ),
        in_specs=[anywhere, anywhere, anywhere, scalars, scalars, vector, vector],
        out_specs=(vector, scalars),
        scratch_shapes=[
            pltpu.VMEM((2, depth + 4, width, length), bf16),
            pltpu.VMEM((depth, width, length), f32),
            pltpu.VMEM((depth, width, length), f32),
            pltpu.VMEM((2, depth + 4, width, length), f32),
            pltpu.VMEM((2, depth + 2, width, length), f32),
            pltpu.VMEM((2, 2, width - width // 2, length), f32),
            pltpu.VMEM((2, width, length), f32),
            pltpu.VMEM((SUMS, 8, length), f32),
            pltpu.VMEM((slabs, SUMS, 128), f32),
            pltpu.VMEM((depth, 2, width, length), f32),
            pltpu.VMEM((nodes, depth, 2, block, length), f32),
            pltpu.VMEM((nodes, 8, 128), f32),
            dma((3,)),
            dma((2,)),
            dma((2,)),
            dma((2,)),
            dma((2,)),
            dma((2,)),
            dma((2,)),
            dma((slabs,)),
            dma((slabs,)),
            dma((nodes,)),
            dma((nodes,)),
            dma((nodes, depth)),
            dma((nodes, depth)),
        ],
        compiler_params=pltpu.CompilerParams(
            collective_id=0, has_side_effects=True, vmem_limit_bytes=40 * 1024 * 1024
        ),
    )(
        warm_start,
        probes,
        potential,
        shift_points,
        quad_weights,
        jnp.asarray(ring_matrix(width, 0.0)),
        jnp.asarray(ring_matrix(length, -90.0)),
    )


def solution(mesh):
    return jax.shard_map(
        functools.partial(per_device, mesh.shape["node"], mesh.shape["grid"]),
        mesh=mesh,
        in_specs=(
            P(None, "grid", None, None),
            P("grid", None, None),
            P("node", None, None, "grid", None, None),
            P("node", None),
            P("node", None),
        ),
        out_specs=(P(None, None, None, "grid", "node", None), P()),
        check_vma=False,
    )
```

```python
import functools

import jax
import jax.numpy as jnp
import ml_dtypes
import numpy as np
from jax import lax
from jax.experimental import pallas as pl
from jax.experimental.pallas import tpu as pltpu
from jax.sharding import PartitionSpec as P

MESH = pl.DeviceIdType.MESH
SUMS = 16
CHUNK = 32


def ring_matrix(size, diagonal):
    matrix = np.zeros((size, size), np.float32)
    at = np.arange(size)
    for step, weight in ((1, 16.0), (2, -1.0)):
        matrix[at, (at + step) % size] += weight
        matrix[at, (at - step) % size] += weight
    matrix[at, at] += diagonal
    return matrix.astype(ml_dtypes.bfloat16)


def cmul(a, b):
    return a[0] * b[0] - a[1] * b[1], a[0] * b[1] + a[1] * b[0]


def cdiv(a, b):
    size = b[0] * b[0] + b[1] * b[1]
    return (a[0] * b[0] + a[1] * b[1]) / size, (a[1] * b[0] - a[0] * b[1]) / size


def fold(values):
    rows, cols = values.shape
    return jnp.sum(values.reshape(rows // 8, 8, cols), axis=0)


def kernel(
    nodes,
    slabs,
    warm,
    probes,
    potential,
    shift_hbm,
    weight_hbm,
    along_x_hbm,
    along_y_hbm,
    moments,
    trace,
    xbuf,
    bbuf,
    vbuf,
    rbuf,
    qbuf,
    plane,
    acc,
    sums,
    far_out,
    far_in,
    edge_out,
    edge_in,
    xwide,
    peer_x,
    peer_r,
    peer_q,
    notes,
    shift_ref,
    weight_ref,
    along_x,
    along_y,
    local_sem,
    x_send,
    x_recv,
    r_send,
    r_recv,
    q_send,
    q_recv,
    s_send,
    s_recv,
    n_send,
    n_recv,
    g_send,
    g_recv,
    e_send,
    e_recv,
):
    node, slab = lax.axis_index("node"), lax.axis_index("grid")
    depth, width, length = bbuf.shape
    half = width // 2
    block = width // nodes
    above = (node, lax.rem(slab + 1, slabs))
    below = (node, lax.rem(slab + slabs - 1, slabs))

    loads = [
        pltpu.make_async_copy(warm.at[0, 0], xbuf.at[:, 2 : depth + 2], local_sem.at[0]),
        pltpu.make_async_copy(probes.at[0], bbuf, local_sem.at[1]),
        pltpu.make_async_copy(potential, vbuf, local_sem.at[2]),
        pltpu.make_async_copy(shift_hbm, shift_ref, local_sem.at[3]),
        pltpu.make_async_copy(weight_hbm, weight_ref, local_sem.at[4]),
        pltpu.make_async_copy(along_x_hbm, along_x, local_sem.at[5]),
        pltpu.make_async_copy(along_y_hbm, along_y, local_sem.at[6]),
    ]
    for load in loads:
        load.start()

    barrier = pltpu.get_barrier_semaphore()
    for k in range(1, slabs):
        pl.semaphore_signal(
            barrier, inc=1, device_id=(node, lax.rem(slab + k, slabs)), device_id_type=MESH
        )
    for k in range(1, nodes):
        pl.semaphore_signal(
            barrier, inc=1, device_id=(lax.rem(node + k, nodes), slab), device_id_type=MESH
        )
    pl.semaphore_wait(barrier, slabs + nodes - 2)

    def send(source, target, send_sem, recv_sem, device):
        copy = pltpu.make_async_remote_copy(
            src_ref=source,
            dst_ref=target,
            send_sem=send_sem,
            recv_sem=recv_sem,
            device_id=device,
            device_id_type=MESH,
        )
        copy.start()
        return copy

    x_down = send(
        warm.at[0, 0, :, 0:2], xbuf.at[:, depth + 2 : depth + 4], x_send.at[0], x_recv.at[0], below
    )
    x_up = send(warm.at[0, 0, :, depth - 2 : depth], xbuf.at[:, 0:2], x_send.at[1], x_recv.at[1], above)

    groups = ((2, depth - 2), (0, 2), (depth - 2, depth))
    early = {}

    def share_rows(kind, source, target, offset, group):
        first, last = groups[group]
        slot = 3 * kind + group
        step = 16 if block % 16 == 0 else 8
        copies = []
        for k in range(1, nodes):
            peer = lax.rem(node + k, nodes)
            rows = pl.ds(pl.multiple_of(peer * block, step), block)
            copies.append(
                send(
                    source.at[:, first + offset : last + offset, rows, :],
                    target.at[k, :, first:last],
                    e_send.at[k, slot],
                    e_recv.at[k, slot],
                    (peer, slab),
                )
            )
        early[kind, group] = copies

    narrow = block % 16 == 0
    if narrow:
        for group in range(3):
            share_rows(0, warm.at[0, 0], peer_x, 0, group)

    acc[...] = jnp.zeros_like(acc)
    qbuf[:, depth : depth + 2, half:, :] = jnp.zeros((2, 2, width - half, length), jnp.float32)
    for load in loads:
        load.wait()
    shift = shift_ref[0, 0], shift_ref[0, 1]

    def dot(a, b):
        return jnp.dot(a, b, preferred_element_type=jnp.float32)

    def in_plane_exact(p):
        for part in range(2):
            field = xbuf[part, p + 2]
            plane[part] = dot(field, along_y[...]) + dot(along_x[...], field)

    def in_plane(source, p):
        for part in range(2):
            field = source[part, p]
            high = field.astype(jnp.bfloat16)
            low = (field - high.astype(jnp.float32)).astype(jnp.bfloat16)
            plane[part] = (dot(high, along_y[...]) + dot(low, along_y[...])) + (
                dot(along_x[...], high) + dot(along_x[...], low)
            )

    def apply(field, stencil, local):
        diagonal = shift[0] - local
        return (
            diagonal * field[0] - shift[1] * field[1] + stencil[0] * (1.0 / 24.0),
            diagonal * field[1] + shift[1] * field[0] + stencil[1] * (1.0 / 24.0),
        )

    def in_chunks(first, terms):
        count = terms[1]

        def step(i, totals):
            rows = pl.ds(pl.multiple_of(i * CHUNK, CHUNK), CHUNK)
            values = terms[0](rows)
            return tuple(total + fold(value) for total, value in zip(totals, values))

        zero = jnp.zeros((8, length), jnp.float32)
        totals = lax.fori_loop(0, width // CHUNK, step, (zero,) * count)
        for i, total in enumerate(totals):
            acc[first + i] += total

    def residual_plane(p, carry):
        in_plane_exact(p)

        def terms(rows):
            stencil, field = [], []
            for part in range(2):
                at = [xbuf[part, p + j, rows, :].astype(jnp.float32) for j in range(5)]
                stencil.append(plane[part, rows, :] + 16.0 * (at[1] + at[3]) - (at[0] + at[4]))
                field.append(at[2])
            source = bbuf[p, rows, :]
            image = apply(field, stencil, vbuf[p, rows, :])
            r = source - image[0], -image[1]
            if not narrow:
                for part in range(2):
                    xwide[part, p, rows, :] = field[part]
            rbuf[0, p + 2, rows, :] = r[0]
            rbuf[1, p + 2, rows, :] = r[1]
            return (
                r[0] * r[0] - r[1] * r[1],
                2.0 * r[0] * r[1],
                source * field[0],
                source * field[1],
                source * r[0],
                source * r[1],
            )

        in_chunks(0, (terms, 6))
        return carry

    def image_plane(p, carry):
        in_plane(rbuf, p + 2)

        def terms(rows):
            stencil, field = [], []
            for part in range(2):
                at = [rbuf[part, p + j, rows, :] for j in range(5)]
                stencil.append(plane[part, rows, :] + 16.0 * (at[1] + at[3]) - (at[0] + at[4]))
                field.append(at[2])
            source = bbuf[p, rows, :]
            q = apply(field, stencil, vbuf[p, rows, :])
            qbuf[0, p, rows, :] = q[0]
            qbuf[1, p, rows, :] = q[1]
            return (
                *cmul(field, q),
                q[0] * q[0] - q[1] * q[1],
                2.0 * q[0] * q[1],
                source * q[0],
                source * q[1],
            )

        in_chunks(6, (terms, 6))
        return carry

    def energy_plane(p, carry):
        in_plane(qbuf, p)

        def terms(rows):
            stencil, field = [], []
            for part in range(2):
                stencil.append(
                    plane[part, rows, :]
                    + 32.0 * qbuf[part, p + 1, rows, :]
                    - 2.0 * qbuf[part, p + 2, rows, :]
                )
                field.append(qbuf[part, p, rows, :])
            return cmul(field, apply(field, stencil, vbuf[p, rows, :]))

        in_chunks(12, (terms, 2))
        return carry

    def narrowed(source, target):
        target[...] = source[...].astype(jnp.bfloat16)

    def widened(source, target):
        target[...] = source[...].astype(jnp.float32)

    def shared(group):
        if not narrow:
            share_rows(0, xwide, peer_x, 0, group)
        share_rows(1, rbuf, peer_r, 2, group)

    with jax.named_scope("residual"):
        lax.fori_loop(2, depth - 2, residual_plane, 0)
        shared(0)
        x_up.wait_recv()
        x_down.wait_recv()
        lax.fori_loop(0, 2, residual_plane, 0)
        near_down = send(
            rbuf.at[:, 2], rbuf.at[:, depth + 2], r_send.at[0], r_recv.at[0], below
        )
        narrowed(rbuf.at[:, 3], far_out.at[0])
        far_down = send(far_out.at[0], far_in.at[0], g_send.at[0], g_recv.at[0], below)
        lax.fori_loop(depth - 2, depth, residual_plane, 0)
        near_up = send(rbuf.at[:, depth + 1], rbuf.at[:, 1], r_send.at[1], r_recv.at[1], above)
        narrowed(rbuf.at[:, depth], far_out.at[1])
        far_up = send(far_out.at[1], far_in.at[1], g_send.at[1], g_recv.at[1], above)
        shared(1)
        shared(2)

    with jax.named_scope("image"):
        lax.fori_loop(2, depth - 2, image_plane, 0)
        share_rows(2, qbuf, peer_q, 0, 0)
        near_up.wait_recv()
        far_up.wait_recv()
        widened(far_in.at[1], rbuf.at[:, 0])
        lax.fori_loop(0, 2, image_plane, 0)
        narrowed(qbuf.at[:, 0:2, 0:half], edge_out.at[0])
        q_down = send(edge_out.at[0], edge_in.at[0], q_send.at[0], q_recv.at[0], below)
        near_down.wait_recv()
        far_down.wait_recv()
        widened(far_in.at[0], rbuf.at[:, depth + 3])
        lax.fori_loop(depth - 2, depth, image_plane, 0)
        narrowed(qbuf.at[:, depth - 2 : depth, half:width], edge_out.at[1])
        q_up = send(edge_out.at[1], edge_in.at[1], q_send.at[1], q_recv.at[1], above)
        share_rows(2, qbuf, peer_q, 0, 1)
        share_rows(2, qbuf, peer_q, 0, 2)

    with jax.named_scope("energy"):
        lax.fori_loop(0, depth - 2, energy_plane, 0)
        q_down.wait_recv()
        widened(edge_in.at[0], qbuf.at[:, depth : depth + 2, 0:half])
        lax.fori_loop(depth - 2, depth, energy_plane, 0)
        q_up.wait_recv()

        def crossing(i, totals):
            start = i * CHUNK
            mine = pl.ds(pl.multiple_of(half + start, CHUNK), CHUNK)
            theirs = pl.ds(pl.multiple_of(start, CHUNK), CHUNK)
            near = [edge_in[1, part, 1, theirs, :].astype(jnp.float32) for part in range(2)]
            far = [edge_in[1, part, 0, theirs, :].astype(jnp.float32) for part in range(2)]
            zeroth = [qbuf[part, 0, mine, :] for part in range(2)]
            first = [qbuf[part, 1, mine, :] for part in range(2)]
            one = cmul(zeroth, [32.0 * near[part] - 2.0 * far[part] for part in range(2)])
            two = cmul(first, near)
            return tuple(
                totals[part] + fold((one[part] - 2.0 * two[part]) * (1.0 / 24.0)) for part in range(2)
            )

        zero = jnp.zeros((8, length), jnp.float32)
        totals = lax.fori_loop(0, half // CHUNK, crossing, (zero, zero))
        acc[12] += totals[0]
        acc[13] += totals[1]

    with jax.named_scope("scalars"):
        partial = jnp.sum(acc[...], axis=1)
        lanes = partial[:, 0:128]
        for at in range(128, length, 128):
            lanes = lanes + partial[:, at : at + 128]
        sums[0] = lanes
        scalar_copies = [
            send(
                sums.at[0],
                sums.at[k],
                s_send.at[k],
                s_recv.at[k],
                (node, lax.rem(slab + k, slabs)),
            )
            for k in range(1, slabs)
        ]
        for copy in scalar_copies:
            copy.wait_recv()
        total = jnp.zeros((SUMS, 128), jnp.float32)
        for owner in range(slabs):
            total = total + sums[lax.rem(slab - owner + slabs, slabs)]
        total = jnp.broadcast_to(jnp.sum(total, axis=1, keepdims=True), (SUMS, length))
        pair = lambda i: (total[i : i + 1], total[i + 1 : i + 2])
        s0, t0, t1, s1, s2, t2, s3 = (pair(i) for i in range(0, 14, 2))
        step0 = cdiv(s0, s1)
        square = cmul(step0, step0)
        norm1 = cmul(square, s2)
        norm1 = norm1[0] - s0[0], norm1[1] - s0[1]
        ratio = cdiv(norm1, s0)
        grow = ratio[0] + 1.0, ratio[1]
        one = cmul(cmul(grow, grow), s1)
        two = cmul(cmul(grow, step0), s2)
        three = cmul(square, s3)
        step1 = cdiv(
            norm1, (one[0] - 2.0 * two[0] + three[0], one[1] - 2.0 * two[1] + three[1])
        )
        coef_r = cmul(step1, grow)
        coef_r = coef_r[0] + step0[0], coef_r[1] + step0[1]
        coef_q = cmul(step1, step0)
        coef_q = -coef_q[0], -coef_q[1]
        inner_r, inner_q = cmul(coef_r, t1), cmul(coef_q, t2)
        inner = t0[0] + inner_r[0] + inner_q[0], t0[1] + inner_r[1] + inner_q[1]
        weight = weight_ref[0, 0], weight_ref[0, 1]
        share = cmul(weight, inner)
        following = cmul(weight, ((shift[0] - 4.0) * 0.2, shift[1] * 0.2))
        row = lax.broadcasted_iota(jnp.int32, (16, 128), 0)
        note = jnp.zeros((16, 128), jnp.float32)
        entries = (*weight, *following, *(v[:, 0:128] for v in (*share, *coef_r, *coef_q)))
        for i, entry in enumerate(entries):
            note = jnp.where(row == i, entry, note)
        notes[0] = note
        note_copies = [
            send(notes.at[0], notes.at[k], n_send.at[k], n_recv.at[k], (lax.rem(node + k, nodes), slab))
            for k in range(1, nodes)
        ]

    with jax.named_scope("moments"):
        for copy in note_copies:
            copy.wait_recv()
        whole_trace = jnp.zeros((16, 128), jnp.float32)
        for owner in range(nodes):
            whole_trace = whole_trace + notes[lax.rem(node - owner + nodes, nodes)]
        lane = lax.broadcasted_iota(jnp.int32, (16, 128), 1)
        for part in range(2):
            trace[part] = jnp.sum(jnp.where((row == 4 + part) & (lane == 0), whole_trace, 0.0))
        factors = []
        for k in range(nodes):
            first_lane = jnp.where(lane == 0, notes[k], 0.0)
            wide = jnp.broadcast_to(jnp.sum(first_lane, axis=1, keepdims=True), (16, length))
            factors.append([(wide[i : i + 1], wide[i + 1 : i + 2]) for i in (0, 2, 6, 8)])
        piece = 16 if narrow else 8

        def moment_plane(p, carry):
            def step(i, inner_carry):
                there = pl.ds(pl.multiple_of(i * piece, piece), piece)
                here = pl.ds(pl.multiple_of(node * block + i * piece, piece), piece)
                values = [None] * 4
                for k in range(nodes):
                    if k:
                        x, r, q = (
                            [ref[k, part, p, there, :] for part in range(2)]
                            for ref in (peer_x, peer_r, peer_q)
                        )
                    else:
                        if narrow:
                            x = [xbuf[part, p + 2, here, :] for part in range(2)]
                        else:
                            x = [xwide[part, p, here, :] for part in range(2)]
                        r = [rbuf[part, p + 2, here, :] for part in range(2)]
                        q = [qbuf[part, p, here, :] for part in range(2)]
                    along_r, along_q = cmul(factors[k][2], r), cmul(factors[k][3], q)
                    field = [
                        x[part].astype(jnp.float32) + along_r[part] + along_q[part]
                        for part in range(2)
                    ]
                    for degree in range(2):
                        term = cmul(factors[k][degree], field)
                        for part in range(2):
                            at = 2 * degree + part
                            values[at] = term[part] if k == 0 else values[at] + term[part]
                for degree in range(2):
                    for part in range(2):
                        moments[degree, 0, part, p, there, :] = values[2 * degree + part]
                return inner_carry

            lax.fori_loop(0, block // piece, step, 0)
            return carry

        for group, (first, last) in enumerate(groups):
            for kind in range(3):
                for copy in early[kind, group]:
                    copy.wait_recv()
            lax.fori_loop(first, last, moment_plane, 0)

    early_copies = [copy for copies in early.values() for copy in copies]
    for copy in [x_down, x_up, near_down, near_up, far_down, far_up, q_down, q_up]:
        copy.wait_send()
    for copy in [*scalar_copies, *note_copies, *early_copies]:
        copy.wait_send()


def per_device(nodes, slabs, probes, potential, warm_start, shift_points, quad_weights):
    depth, width, length = potential.shape
    block = width // nodes
    narrow = block % 16 == 0
    f32, bf16 = jnp.float32, jnp.bfloat16
    anywhere = pl.BlockSpec(memory_space=pltpu.HBM)
    scalars = pl.BlockSpec(memory_space=pltpu.SMEM)
    vector = pl.BlockSpec(memory_space=pltpu.VMEM)
    dma = pltpu.SemaphoreType.DMA
    return pl.pallas_call(
        functools.partial(kernel, nodes, slabs),
        out_shape=(
            jax.ShapeDtypeStruct((2, 1, 2, depth, block, length), f32),
            jax.ShapeDtypeStruct((2,), f32),
        ),
        in_specs=[anywhere] * 7,
        out_specs=(vector, scalars),
        scratch_shapes=[
            pltpu.VMEM((2, depth + 4, width, length), bf16),
            pltpu.VMEM((depth, width, length), f32),
            pltpu.VMEM((depth, width, length), f32),
            pltpu.VMEM((2, depth + 4, width, length), f32),
            pltpu.VMEM((2, depth + 2, width, length), f32),
            pltpu.VMEM((2, width, length), f32),
            pltpu.VMEM((SUMS, 8, length), f32),
            pltpu.VMEM((slabs, SUMS, 128), f32),
            pltpu.VMEM((2, 2, width, length), bf16),
            pltpu.VMEM((2, 2, width, length), bf16),
            pltpu.VMEM((2, 2, 2, width // 2, length), bf16),
            pltpu.VMEM((2, 2, 2, width // 2, length), bf16),
            pltpu.VMEM((8, 128) if narrow else (2, depth, width, length), f32),
            pltpu.VMEM((nodes, 2, depth, block, length), bf16 if narrow else f32),
            pltpu.VMEM((nodes, 2, depth, block, length), f32),
            pltpu.VMEM((nodes, 2, depth, block, length), f32),
            pltpu.VMEM((nodes, 16, 128), f32),
            pltpu.SMEM((1, 2), f32),
            pltpu.SMEM((1, 2), f32),
            pltpu.VMEM((width, width), bf16),
            pltpu.VMEM((length, length), bf16),
            dma((7,)),
            dma((2,)),
            dma((2,)),
            dma((2,)),
            dma((2,)),
            dma((2,)),
            dma((2,)),
            dma((slabs,)),
            dma((slabs,)),
            dma((nodes,)),
            dma((nodes,)),
            dma((2,)),
            dma((2,)),
            dma((nodes, 9)),
            dma((nodes, 9)),
        ],
        compiler_params=pltpu.CompilerParams(
            collective_id=0, has_side_effects=True, vmem_limit_bytes=40 * 1024 * 1024
        ),
    )(
        warm_start,
        probes,
        potential,
        shift_points,
        quad_weights,
        jnp.asarray(ring_matrix(width, 0.0)),
        jnp.asarray(ring_matrix(length, -90.0)),
    )


def solution(mesh):
    return jax.shard_map(
        functools.partial(per_device, mesh.shape["node"], mesh.shape["grid"]),
        mesh=mesh,
        in_specs=(
            P(None, "grid", None, None),
            P("grid", None, None),
            P("node", None, None, "grid", None, None),
            P("node", None),
            P("node", None),
        ),
        out_specs=(P(None, None, None, "grid", "node", None), P()),
        check_vma=False,
    )
```

```python
import functools

import jax
import jax.numpy as jnp
import ml_dtypes
import numpy as np
from jax import lax
from jax.experimental import pallas as pl
from jax.experimental.pallas import tpu as pltpu
from jax.sharding import PartitionSpec as P

MESH = pl.DeviceIdType.MESH
SUMS = 16
CHUNK = 32


def ring_matrix(size, diagonal):
    matrix = np.zeros((size, size), np.float32)
    at = np.arange(size)
    for step, weight in ((1, 16.0), (2, -1.0)):
        matrix[at, (at + step) % size] += weight
        matrix[at, (at - step) % size] += weight
    matrix[at, at] += diagonal
    return matrix.astype(ml_dtypes.bfloat16)


def cmul(a, b):
    return a[0] * b[0] - a[1] * b[1], a[0] * b[1] + a[1] * b[0]


def cdiv(a, b):
    size = b[0] * b[0] + b[1] * b[1]
    return (a[0] * b[0] + a[1] * b[1]) / size, (a[1] * b[0] - a[0] * b[1]) / size


def fold(values):
    rows, cols = values.shape
    return jnp.sum(values.reshape(rows // 8, 8, cols), axis=0)


def kernel(
    nodes,
    slabs,
    warm,
    probes,
    potential,
    shift_hbm,
    weight_hbm,
    along_x_hbm,
    along_y_hbm,
    moments,
    trace,
    xbuf,
    bbuf,
    vbuf,
    rbuf,
    qbuf,
    plane,
    acc,
    sums,
    far_out,
    far_in,
    edge_out,
    edge_in,
    xwide,
    peer_x,
    peer_r,
    peer_q,
    late,
    peer_late,
    notes,
    shift_ref,
    weight_ref,
    along_x,
    along_y,
    local_sem,
    x_send,
    x_recv,
    r_send,
    r_recv,
    q_send,
    q_recv,
    s_send,
    s_recv,
    n_send,
    n_recv,
    g_send,
    g_recv,
    e_send,
    e_recv,
):
    node, slab = lax.axis_index("node"), lax.axis_index("grid")
    depth, width, length = bbuf.shape
    half = width // 2
    block = width // nodes
    above = (node, lax.rem(slab + 1, slabs))
    below = (node, lax.rem(slab + slabs - 1, slabs))

    loads = [
        pltpu.make_async_copy(warm.at[0, 0], xbuf.at[:, 2 : depth + 2], local_sem.at[0]),
        pltpu.make_async_copy(probes.at[0], bbuf, local_sem.at[1]),
        pltpu.make_async_copy(potential, vbuf, local_sem.at[2]),
        pltpu.make_async_copy(shift_hbm, shift_ref, local_sem.at[3]),
        pltpu.make_async_copy(weight_hbm, weight_ref, local_sem.at[4]),
        pltpu.make_async_copy(along_x_hbm, along_x, local_sem.at[5]),
        pltpu.make_async_copy(along_y_hbm, along_y, local_sem.at[6]),
    ]
    for load in loads:
        load.start()

    barrier = pltpu.get_barrier_semaphore()
    for k in range(1, slabs):
        pl.semaphore_signal(
            barrier, inc=1, device_id=(node, lax.rem(slab + k, slabs)), device_id_type=MESH
        )
    for k in range(1, nodes):
        pl.semaphore_signal(
            barrier, inc=1, device_id=(lax.rem(node + k, nodes), slab), device_id_type=MESH
        )
    pl.semaphore_wait(barrier, slabs + nodes - 2)

    def send(source, target, send_sem, recv_sem, device):
        copy = pltpu.make_async_remote_copy(
            src_ref=source,
            dst_ref=target,
            send_sem=send_sem,
            recv_sem=recv_sem,
            device_id=device,
            device_id_type=MESH,
        )
        copy.start()
        return copy

    x_down = send(
        warm.at[0, 0, :, 0:2], xbuf.at[:, depth + 2 : depth + 4], x_send.at[0], x_recv.at[0], below
    )
    x_up = send(warm.at[0, 0, :, depth - 2 : depth], xbuf.at[:, 0:2], x_send.at[1], x_recv.at[1], above)

    groups = ((2, depth - 2), (0, 2), (depth - 2, depth))
    early = {}

    def share_rows(kind, source, target, offset, group):
        first, last = groups[group]
        slot = 2 * kind + group
        step = 16 if block % 16 == 0 else 8
        copies = []
        for k in range(1, nodes):
            peer = lax.rem(node + k, nodes)
            rows = pl.ds(pl.multiple_of(peer * block, step), block)
            copies.append(
                send(
                    source.at[:, first + offset : last + offset, rows, :],
                    target.at[k, :, first:last],
                    e_send.at[k, slot],
                    e_recv.at[k, slot],
                    (peer, slab),
                )
            )
        early[kind, group] = copies

    narrow = block % 16 == 0
    if narrow:
        for group in range(2):
            share_rows(0, warm.at[0, 0], peer_x, 0, group)

    acc[...] = jnp.zeros_like(acc)
    qbuf[:, depth : depth + 2, half:, :] = jnp.zeros((2, 2, width - half, length), jnp.float32)
    for load in loads:
        load.wait()
    shift = shift_ref[0, 0], shift_ref[0, 1]

    def dot(a, b):
        return jnp.dot(a, b, preferred_element_type=jnp.float32)

    def in_plane_exact(p):
        for part in range(2):
            field = xbuf[part, p + 2]
            plane[part] = dot(field, along_y[...]) + dot(along_x[...], field)

    def in_plane(source, p):
        for part in range(2):
            field = source[part, p]
            high = field.astype(jnp.bfloat16)
            low = (field - high.astype(jnp.float32)).astype(jnp.bfloat16)
            plane[part] = (dot(high, along_y[...]) + dot(low, along_y[...])) + (
                dot(along_x[...], high) + dot(along_x[...], low)
            )

    def apply(field, stencil, local):
        diagonal = shift[0] - local
        return (
            diagonal * field[0] - shift[1] * field[1] + stencil[0] * (1.0 / 24.0),
            diagonal * field[1] + shift[1] * field[0] + stencil[1] * (1.0 / 24.0),
        )

    def in_chunks(first, terms):
        count = terms[1]

        def step(i, totals):
            rows = pl.ds(pl.multiple_of(i * CHUNK, CHUNK), CHUNK)
            values = terms[0](rows)
            return tuple(total + fold(value) for total, value in zip(totals, values))

        zero = jnp.zeros((8, length), jnp.float32)
        totals = lax.fori_loop(0, width // CHUNK, step, (zero,) * count)
        for i, total in enumerate(totals):
            acc[first + i] += total

    def residual_plane(p, carry):
        in_plane_exact(p)

        def terms(rows):
            stencil, field = [], []
            for part in range(2):
                at = [xbuf[part, p + j, rows, :].astype(jnp.float32) for j in range(5)]
                stencil.append(plane[part, rows, :] + 16.0 * (at[1] + at[3]) - (at[0] + at[4]))
                field.append(at[2])
            source = bbuf[p, rows, :]
            image = apply(field, stencil, vbuf[p, rows, :])
            r = source - image[0], -image[1]
            if not narrow:
                for part in range(2):
                    xwide[part, p, rows, :] = field[part]
            rbuf[0, p + 2, rows, :] = r[0]
            rbuf[1, p + 2, rows, :] = r[1]
            return (
                r[0] * r[0] - r[1] * r[1],
                2.0 * r[0] * r[1],
                source * field[0],
                source * field[1],
                source * r[0],
                source * r[1],
            )

        in_chunks(0, (terms, 6))
        return carry

    def image_plane(p, carry):
        in_plane(rbuf, p + 2)

        def terms(rows):
            stencil, field = [], []
            for part in range(2):
                at = [rbuf[part, p + j, rows, :] for j in range(5)]
                stencil.append(plane[part, rows, :] + 16.0 * (at[1] + at[3]) - (at[0] + at[4]))
                field.append(at[2])
            source = bbuf[p, rows, :]
            q = apply(field, stencil, vbuf[p, rows, :])
            qbuf[0, p, rows, :] = q[0]
            qbuf[1, p, rows, :] = q[1]
            return (
                *cmul(field, q),
                q[0] * q[0] - q[1] * q[1],
                2.0 * q[0] * q[1],
                source * q[0],
                source * q[1],
            )

        in_chunks(6, (terms, 6))
        return carry

    def energy_plane(p, carry):
        in_plane(qbuf, p)

        def terms(rows):
            stencil, field = [], []
            for part in range(2):
                stencil.append(
                    plane[part, rows, :]
                    + 32.0 * qbuf[part, p + 1, rows, :]
                    - 2.0 * qbuf[part, p + 2, rows, :]
                )
                field.append(qbuf[part, p, rows, :])
            return cmul(field, apply(field, stencil, vbuf[p, rows, :]))

        in_chunks(12, (terms, 2))
        return carry

    def narrowed(source, target):
        target[...] = source[...].astype(jnp.bfloat16)

    def widened(source, target):
        target[...] = source[...].astype(jnp.float32)

    def shared(group):
        if not narrow:
            share_rows(0, xwide, peer_x, 0, group)
        share_rows(1, rbuf, peer_r, 2, group)

    with jax.named_scope("residual"):
        lax.fori_loop(2, depth - 2, residual_plane, 0)
        shared(0)
        x_up.wait_recv()
        x_down.wait_recv()
        lax.fori_loop(0, 2, residual_plane, 0)
        near_down = send(
            rbuf.at[:, 2], rbuf.at[:, depth + 2], r_send.at[0], r_recv.at[0], below
        )
        narrowed(rbuf.at[:, 3], far_out.at[0])
        far_down = send(far_out.at[0], far_in.at[0], g_send.at[0], g_recv.at[0], below)
        lax.fori_loop(depth - 2, depth, residual_plane, 0)
        near_up = send(rbuf.at[:, depth + 1], rbuf.at[:, 1], r_send.at[1], r_recv.at[1], above)
        narrowed(rbuf.at[:, depth], far_out.at[1])
        far_up = send(far_out.at[1], far_in.at[1], g_send.at[1], g_recv.at[1], above)
        shared(1)

    with jax.named_scope("image"):
        lax.fori_loop(2, depth - 2, image_plane, 0)
        share_rows(2, qbuf, peer_q, 0, 0)
        near_up.wait_recv()
        far_up.wait_recv()
        widened(far_in.at[1], rbuf.at[:, 0])
        lax.fori_loop(0, 2, image_plane, 0)
        narrowed(qbuf.at[:, 0:2, 0:half], edge_out.at[0])
        q_down = send(edge_out.at[0], edge_in.at[0], q_send.at[0], q_recv.at[0], below)
        near_down.wait_recv()
        far_down.wait_recv()
        widened(far_in.at[0], rbuf.at[:, depth + 3])
        lax.fori_loop(depth - 2, depth, image_plane, 0)
        narrowed(qbuf.at[:, depth - 2 : depth, half:width], edge_out.at[1])
        q_up = send(edge_out.at[1], edge_in.at[1], q_send.at[1], q_recv.at[1], above)
        share_rows(2, qbuf, peer_q, 0, 1)

    with jax.named_scope("energy"):
        lax.fori_loop(0, depth - 2, energy_plane, 0)
        q_down.wait_recv()
        widened(edge_in.at[0], qbuf.at[:, depth : depth + 2, 0:half])
        lax.fori_loop(depth - 2, depth, energy_plane, 0)
        q_up.wait_recv()

        def crossing(i, totals):
            start = i * CHUNK
            mine = pl.ds(pl.multiple_of(half + start, CHUNK), CHUNK)
            theirs = pl.ds(pl.multiple_of(start, CHUNK), CHUNK)
            near = [edge_in[1, part, 1, theirs, :].astype(jnp.float32) for part in range(2)]
            far = [edge_in[1, part, 0, theirs, :].astype(jnp.float32) for part in range(2)]
            zeroth = [qbuf[part, 0, mine, :] for part in range(2)]
            first = [qbuf[part, 1, mine, :] for part in range(2)]
            one = cmul(zeroth, [32.0 * near[part] - 2.0 * far[part] for part in range(2)])
            two = cmul(first, near)
            return tuple(
                totals[part] + fold((one[part] - 2.0 * two[part]) * (1.0 / 24.0)) for part in range(2)
            )

        zero = jnp.zeros((8, length), jnp.float32)
        totals = lax.fori_loop(0, half // CHUNK, crossing, (zero, zero))
        acc[12] += totals[0]
        acc[13] += totals[1]

    with jax.named_scope("scalars"):
        partial = jnp.sum(acc[...], axis=1)
        lanes = partial[:, 0:128]
        for at in range(128, length, 128):
            lanes = lanes + partial[:, at : at + 128]
        sums[0] = lanes
        scalar_copies = [
            send(
                sums.at[0],
                sums.at[k],
                s_send.at[k],
                s_recv.at[k],
                (node, lax.rem(slab + k, slabs)),
            )
            for k in range(1, slabs)
        ]
        for copy in scalar_copies:
            copy.wait_recv()
        total = jnp.zeros((SUMS, 128), jnp.float32)
        for owner in range(slabs):
            total = total + sums[lax.rem(slab - owner + slabs, slabs)]
        total = jnp.broadcast_to(jnp.sum(total, axis=1, keepdims=True), (SUMS, length))
        pair = lambda i: (total[i : i + 1], total[i + 1 : i + 2])
        s0, t0, t1, s1, s2, t2, s3 = (pair(i) for i in range(0, 14, 2))
        step0 = cdiv(s0, s1)
        square = cmul(step0, step0)
        norm1 = cmul(square, s2)
        norm1 = norm1[0] - s0[0], norm1[1] - s0[1]
        ratio = cdiv(norm1, s0)
        grow = ratio[0] + 1.0, ratio[1]
        one = cmul(cmul(grow, grow), s1)
        two = cmul(cmul(grow, step0), s2)
        three = cmul(square, s3)
        step1 = cdiv(
            norm1, (one[0] - 2.0 * two[0] + three[0], one[1] - 2.0 * two[1] + three[1])
        )
        coef_r = cmul(step1, grow)
        coef_r = coef_r[0] + step0[0], coef_r[1] + step0[1]
        coef_q = cmul(step1, step0)
        coef_q = -coef_q[0], -coef_q[1]
        inner_r, inner_q = cmul(coef_r, t1), cmul(coef_q, t2)
        inner = t0[0] + inner_r[0] + inner_q[0], t0[1] + inner_r[1] + inner_q[1]
        weight = weight_ref[0, 0], weight_ref[0, 1]
        share = cmul(weight, inner)
        following = cmul(weight, ((shift[0] - 4.0) * 0.2, shift[1] * 0.2))
        row = lax.broadcasted_iota(jnp.int32, (16, 128), 0)
        note = jnp.zeros((16, 128), jnp.float32)
        entries = (*weight, *following, *(v[:, 0:128] for v in (*share, *coef_r, *coef_q)))
        for i, entry in enumerate(entries):
            note = jnp.where(row == i, entry, note)
        notes[0] = note
        note_copies = [
            send(notes.at[0], notes.at[k], n_send.at[k], n_recv.at[k], (lax.rem(node + k, nodes), slab))
            for k in range(1, nodes)
        ]

    with jax.named_scope("moments"):
        late_first = depth - 2
        late_copies = []

        def late_plane(p):
            def step(i, carry):
                rows = pl.ds(pl.multiple_of(i * CHUNK, CHUNK), CHUNK)
                r = rbuf[0, p + 2, rows, :], rbuf[1, p + 2, rows, :]
                q = qbuf[0, p, rows, :], qbuf[1, p, rows, :]
                along_r, along_q = cmul(coef_r, r), cmul(coef_q, q)
                for part in range(2):
                    start = xbuf[part, p + 2, rows, :].astype(jnp.float32)
                    late[p - late_first, part, rows, :] = start + along_r[part] + along_q[part]
                return carry

            lax.fori_loop(0, width // CHUNK, step, 0)

        for p in range(late_first, depth):
            late_plane(p)
            for k in range(1, nodes):
                peer = lax.rem(node + k, nodes)
                late_copies.append(
                    send(
                        late.at[p - late_first, :, pl.ds(pl.multiple_of(peer * block, 8), block), :],
                        peer_late.at[k, p - late_first],
                        e_send.at[k, 6 + p - late_first],
                        e_recv.at[k, 6 + p - late_first],
                        (peer, slab),
                    )
                )

        for copy in note_copies:
            copy.wait_recv()
        whole_trace = jnp.zeros((16, 128), jnp.float32)
        for owner in range(nodes):
            whole_trace = whole_trace + notes[lax.rem(node - owner + nodes, nodes)]
        lane = lax.broadcasted_iota(jnp.int32, (16, 128), 1)
        for part in range(2):
            trace[part] = jnp.sum(jnp.where((row == 4 + part) & (lane == 0), whole_trace, 0.0))
        factors = []
        for k in range(nodes):
            first_lane = jnp.where(lane == 0, notes[k], 0.0)
            wide = jnp.broadcast_to(jnp.sum(first_lane, axis=1, keepdims=True), (16, length))
            factors.append([(wide[i : i + 1], wide[i + 1 : i + 2]) for i in (0, 2, 6, 8)])
        piece = 16 if narrow else 8

        def late_moment_plane(at, carry):
            def step(i, inner_carry):
                there = pl.ds(pl.multiple_of(i * piece, piece), piece)
                here = pl.ds(pl.multiple_of(node * block + i * piece, piece), piece)
                values = [None] * 4
                for k in range(nodes):
                    if k:
                        field = [peer_late[k, at, part, there, :] for part in range(2)]
                    else:
                        field = [late[at, part, here, :] for part in range(2)]
                    for degree in range(2):
                        term = cmul(factors[k][degree], field)
                        for part in range(2):
                            n = 2 * degree + part
                            values[n] = term[part] if k == 0 else values[n] + term[part]
                for degree in range(2):
                    for part in range(2):
                        moments[degree, 0, part, late_first + at, there, :] = values[2 * degree + part]
                return inner_carry

            lax.fori_loop(0, block // piece, step, 0)
            return carry

        def moment_plane(p, carry):
            def step(i, inner_carry):
                there = pl.ds(pl.multiple_of(i * piece, piece), piece)
                here = pl.ds(pl.multiple_of(node * block + i * piece, piece), piece)
                values = [None] * 4
                for k in range(nodes):
                    if k:
                        x, r, q = (
                            [ref[k, part, p, there, :] for part in range(2)]
                            for ref in (peer_x, peer_r, peer_q)
                        )
                    else:
                        if narrow:
                            x = [xbuf[part, p + 2, here, :] for part in range(2)]
                        else:
                            x = [xwide[part, p, here, :] for part in range(2)]
                        r = [rbuf[part, p + 2, here, :] for part in range(2)]
                        q = [qbuf[part, p, here, :] for part in range(2)]
                    along_r, along_q = cmul(factors[k][2], r), cmul(factors[k][3], q)
                    field = [
                        x[part].astype(jnp.float32) + along_r[part] + along_q[part]
                        for part in range(2)
                    ]
                    for degree in range(2):
                        term = cmul(factors[k][degree], field)
                        for part in range(2):
                            at = 2 * degree + part
                            values[at] = term[part] if k == 0 else values[at] + term[part]
                for degree in range(2):
                    for part in range(2):
                        moments[degree, 0, part, p, there, :] = values[2 * degree + part]
                return inner_carry

            lax.fori_loop(0, block // piece, step, 0)
            return carry

        for group, (first, last) in enumerate(groups[:2]):
            for kind in range(3):
                for copy in early[kind, group]:
                    copy.wait_recv()
            lax.fori_loop(first, last, moment_plane, 0)

        for at in range(2):
            for copy in late_copies[at * (nodes - 1) : (at + 1) * (nodes - 1)]:
                copy.wait_recv()
            late_moment_plane(at, 0)

    early_copies = late_copies + [copy for copies in early.values() for copy in copies]
    for copy in [x_down, x_up, near_down, near_up, far_down, far_up, q_down, q_up]:
        copy.wait_send()
    for copy in [*scalar_copies, *note_copies, *early_copies]:
        copy.wait_send()


def per_device(nodes, slabs, probes, potential, warm_start, shift_points, quad_weights):
    depth, width, length = potential.shape
    block = width // nodes
    narrow = block % 16 == 0
    f32, bf16 = jnp.float32, jnp.bfloat16
    anywhere = pl.BlockSpec(memory_space=pltpu.HBM)
    scalars = pl.BlockSpec(memory_space=pltpu.SMEM)
    vector = pl.BlockSpec(memory_space=pltpu.VMEM)
    dma = pltpu.SemaphoreType.DMA
    return pl.pallas_call(
        functools.partial(kernel, nodes, slabs),
        out_shape=(
            jax.ShapeDtypeStruct((2, 1, 2, depth, block, length), f32),
            jax.ShapeDtypeStruct((2,), f32),
        ),
        in_specs=[anywhere] * 7,
        out_specs=(vector, scalars),
        scratch_shapes=[
            pltpu.VMEM((2, depth + 4, width, length), bf16),
            pltpu.VMEM((depth, width, length), f32),
            pltpu.VMEM((depth, width, length), f32),
            pltpu.VMEM((2, depth + 4, width, length), f32),
            pltpu.VMEM((2, depth + 2, width, length), f32),
            pltpu.VMEM((2, width, length), f32),
            pltpu.VMEM((SUMS, 8, length), f32),
            pltpu.VMEM((slabs, SUMS, 128), f32),
            pltpu.VMEM((2, 2, width, length), bf16),
            pltpu.VMEM((2, 2, width, length), bf16),
            pltpu.VMEM((2, 2, 2, width // 2, length), bf16),
            pltpu.VMEM((2, 2, 2, width // 2, length), bf16),
            pltpu.VMEM((8, 128) if narrow else (2, depth, width, length), f32),
            pltpu.VMEM((nodes, 2, depth, block, length), bf16 if narrow else f32),
            pltpu.VMEM((nodes, 2, depth, block, length), f32),
            pltpu.VMEM((nodes, 2, depth, block, length), f32),
            pltpu.VMEM((2, 2, width, length), f32),
            pltpu.VMEM((nodes, 2, 2, block, length), f32),
            pltpu.VMEM((nodes, 16, 128), f32),
            pltpu.SMEM((1, 2), f32),
            pltpu.SMEM((1, 2), f32),
            pltpu.VMEM((width, width), bf16),
            pltpu.VMEM((length, length), bf16),
            dma((7,)),
            dma((2,)),
            dma((2,)),
            dma((2,)),
            dma((2,)),
            dma((2,)),
            dma((2,)),
            dma((slabs,)),
            dma((slabs,)),
            dma((nodes,)),
            dma((nodes,)),
            dma((2,)),
            dma((2,)),
            dma((nodes, 8)),
            dma((nodes, 8)),
        ],
        compiler_params=pltpu.CompilerParams(
            collective_id=0, has_side_effects=True, vmem_limit_bytes=64 * 1024 * 1024
        ),
    )(
        warm_start,
        probes,
        potential,
        shift_points,
        quad_weights,
        jnp.asarray(ring_matrix(width, 0.0)),
        jnp.asarray(ring_matrix(length, -90.0)),
    )


def solution(mesh):
    return jax.shard_map(
        functools.partial(per_device, mesh.shape["node"], mesh.shape["grid"]),
        mesh=mesh,
        in_specs=(
            P(None, "grid", None, None),
            P("grid", None, None),
            P("node", None, None, "grid", None, None),
            P("node", None),
            P("node", None),
        ),
        out_specs=(P(None, None, None, "grid", "node", None), P()),
        check_vma=False,
    )
```

```python
import functools

import jax
import jax.numpy as jnp
import ml_dtypes
import numpy as np
from jax import lax
from jax.experimental import pallas as pl
from jax.experimental.pallas import tpu as pltpu
from jax.sharding import PartitionSpec as P

MESH = pl.DeviceIdType.MESH
SUMS = 16
CHUNK = 32


def ring_matrix(size, diagonal):
    matrix = np.zeros((size, size), np.float32)
    at = np.arange(size)
    for step, weight in ((1, 16.0), (2, -1.0)):
        matrix[at, (at + step) % size] += weight
        matrix[at, (at - step) % size] += weight
    matrix[at, at] += diagonal
    return matrix.astype(ml_dtypes.bfloat16)


def cmul(a, b):
    return a[0] * b[0] - a[1] * b[1], a[0] * b[1] + a[1] * b[0]


def cdiv(a, b):
    size = b[0] * b[0] + b[1] * b[1]
    return (a[0] * b[0] + a[1] * b[1]) / size, (a[1] * b[0] - a[0] * b[1]) / size


def fold(values):
    rows, cols = values.shape
    return jnp.sum(values.reshape(rows // 8, 8, cols), axis=0)


def kernel(
    nodes,
    slabs,
    warm,
    probes,
    potential,
    shift_hbm,
    weight_hbm,
    along_x_hbm,
    along_y_hbm,
    moments,
    trace,
    xbuf,
    bbuf,
    vbuf,
    rbuf,
    qbuf,
    plane,
    acc,
    sums,
    far_out,
    far_in,
    edge_out,
    edge_in,
    xwide,
    peer_x,
    peer_r,
    peer_q,
    late,
    peer_late,
    notes,
    shift_ref,
    weight_ref,
    along_x,
    along_y,
    local_sem,
    x_send,
    x_recv,
    r_send,
    r_recv,
    q_send,
    q_recv,
    s_send,
    s_recv,
    n_send,
    n_recv,
    g_send,
    g_recv,
    e_send,
    e_recv,
):
    node, slab = lax.axis_index("node"), lax.axis_index("grid")
    depth, width, length = bbuf.shape
    half = width // 2
    block = width // nodes
    above = (node, lax.rem(slab + 1, slabs))
    below = (node, lax.rem(slab + slabs - 1, slabs))

    loads = [
        pltpu.make_async_copy(warm.at[0, 0], xbuf.at[:, 2 : depth + 2], local_sem.at[0]),
        pltpu.make_async_copy(probes.at[0], bbuf, local_sem.at[1]),
        pltpu.make_async_copy(potential, vbuf, local_sem.at[2]),
        pltpu.make_async_copy(shift_hbm, shift_ref, local_sem.at[3]),
        pltpu.make_async_copy(weight_hbm, weight_ref, local_sem.at[4]),
        pltpu.make_async_copy(along_x_hbm, along_x, local_sem.at[5]),
        pltpu.make_async_copy(along_y_hbm, along_y, local_sem.at[6]),
    ]
    for load in loads:
        load.start()

    barrier = pltpu.get_barrier_semaphore()
    for k in range(1, slabs):
        pl.semaphore_signal(
            barrier, inc=1, device_id=(node, lax.rem(slab + k, slabs)), device_id_type=MESH
        )
    for k in range(1, nodes):
        pl.semaphore_signal(
            barrier, inc=1, device_id=(lax.rem(node + k, nodes), slab), device_id_type=MESH
        )
    pl.semaphore_wait(barrier, slabs + nodes - 2)

    def send(source, target, send_sem, recv_sem, device):
        copy = pltpu.make_async_remote_copy(
            src_ref=source,
            dst_ref=target,
            send_sem=send_sem,
            recv_sem=recv_sem,
            device_id=device,
            device_id_type=MESH,
        )
        copy.start()
        return copy

    x_down = send(
        warm.at[0, 0, :, 0:2], xbuf.at[:, depth + 2 : depth + 4], x_send.at[0], x_recv.at[0], below
    )
    x_up = send(warm.at[0, 0, :, depth - 2 : depth], xbuf.at[:, 0:2], x_send.at[1], x_recv.at[1], above)

    groups = ((2, depth - 2), (0, 2), (depth - 2, depth))
    early = {}

    def share_rows(kind, source, target, offset, group):
        first, last = groups[group]
        slot = 2 * kind + group
        step = 16 if block % 16 == 0 else 8
        copies = []
        for k in range(1, nodes):
            peer = lax.rem(node + k, nodes)
            rows = pl.ds(pl.multiple_of(peer * block, step), block)
            copies.append(
                send(
                    source.at[:, first + offset : last + offset, rows, :],
                    target.at[k, :, first:last],
                    e_send.at[k, slot],
                    e_recv.at[k, slot],
                    (peer, slab),
                )
            )
        early[kind, group] = copies

    narrow = block % 16 == 0
    if narrow:
        for group in range(2):
            share_rows(0, warm.at[0, 0], peer_x, 0, group)

    acc[...] = jnp.zeros_like(acc)
    qbuf[:, depth : depth + 2, half:, :] = jnp.zeros((2, 2, width - half, length), jnp.float32)
    for load in loads:
        load.wait()
    shift = shift_ref[0, 0], shift_ref[0, 1]

    def dot(a, b):
        return jnp.dot(a, b, preferred_element_type=jnp.float32)

    def in_plane_exact(p):
        for part in range(2):
            field = xbuf[part, p + 2]
            plane[part] = dot(field, along_y[...]) + dot(along_x[...], field)

    def in_plane(source, p):
        for part in range(2):
            field = source[part, p]
            high = field.astype(jnp.bfloat16)
            low = (field - high.astype(jnp.float32)).astype(jnp.bfloat16)
            plane[part] = (dot(high, along_y[...]) + dot(low, along_y[...])) + (
                dot(along_x[...], high) + dot(along_x[...], low)
            )

    def apply(field, stencil, local):
        diagonal = shift[0] - local
        return (
            diagonal * field[0] - shift[1] * field[1] + stencil[0] * (1.0 / 24.0),
            diagonal * field[1] + shift[1] * field[0] + stencil[1] * (1.0 / 24.0),
        )

    def in_chunks(first, terms):
        count = terms[1]

        def step(i, totals):
            rows = pl.ds(pl.multiple_of(i * CHUNK, CHUNK), CHUNK)
            values = terms[0](rows)
            return tuple(total + fold(value) for total, value in zip(totals, values))

        zero = jnp.zeros((8, length), jnp.float32)
        totals = lax.fori_loop(0, width // CHUNK, step, (zero,) * count)
        for i, total in enumerate(totals):
            acc[first + i] += total

    def residual_plane(p, carry):
        in_plane_exact(p)

        def terms(rows):
            stencil, field = [], []
            for part in range(2):
                at = [xbuf[part, p + j, rows, :].astype(jnp.float32) for j in range(5)]
                stencil.append(plane[part, rows, :] + 16.0 * (at[1] + at[3]) - (at[0] + at[4]))
                field.append(at[2])
            source = bbuf[p, rows, :]
            image = apply(field, stencil, vbuf[p, rows, :])
            r = source - image[0], -image[1]
            if not narrow:
                for part in range(2):
                    xwide[part, p, rows, :] = field[part]
            rbuf[0, p + 2, rows, :] = r[0]
            rbuf[1, p + 2, rows, :] = r[1]
            return (
                r[0] * r[0] - r[1] * r[1],
                2.0 * r[0] * r[1],
                source * field[0],
                source * field[1],
                source * r[0],
                source * r[1],
            )

        in_chunks(0, (terms, 6))
        return carry

    def image_plane(p, carry):
        in_plane(rbuf, p + 2)

        def terms(rows):
            stencil, field = [], []
            for part in range(2):
                at = [rbuf[part, p + j, rows, :] for j in range(5)]
                stencil.append(plane[part, rows, :] + 16.0 * (at[1] + at[3]) - (at[0] + at[4]))
                field.append(at[2])
            source = bbuf[p, rows, :]
            q = apply(field, stencil, vbuf[p, rows, :])
            qbuf[0, p, rows, :] = q[0]
            qbuf[1, p, rows, :] = q[1]
            return (
                *cmul(field, q),
                q[0] * q[0] - q[1] * q[1],
                2.0 * q[0] * q[1],
                source * q[0],
                source * q[1],
            )

        in_chunks(6, (terms, 6))
        return carry

    def energy_plane(p, carry):
        in_plane(qbuf, p)

        def terms(rows):
            stencil, field = [], []
            for part in range(2):
                stencil.append(
                    plane[part, rows, :]
                    + 32.0 * qbuf[part, p + 1, rows, :]
                    - 2.0 * qbuf[part, p + 2, rows, :]
                )
                field.append(qbuf[part, p, rows, :])
            return cmul(field, apply(field, stencil, vbuf[p, rows, :]))

        in_chunks(12, (terms, 2))
        return carry

    def narrowed(source, target):
        target[...] = source[...].astype(jnp.bfloat16)

    def widened(source, target):
        target[...] = source[...].astype(jnp.float32)

    def shared(group):
        if not narrow:
            share_rows(0, xwide, peer_x, 0, group)
        share_rows(1, rbuf, peer_r, 2, group)

    with jax.named_scope("residual"):
        lax.fori_loop(2, depth - 2, residual_plane, 0)
        shared(0)
        x_up.wait_recv()
        lax.fori_loop(0, 1, residual_plane, 0)
        near_down = send(
            rbuf.at[:, 2], rbuf.at[:, depth + 2], r_send.at[0], r_recv.at[0], below
        )
        lax.fori_loop(1, 2, residual_plane, 0)
        narrowed(rbuf.at[:, 3], far_out.at[0])
        far_down = send(far_out.at[0], far_in.at[0], g_send.at[0], g_recv.at[0], below)
        x_down.wait_recv()
        lax.fori_loop(depth - 1, depth, residual_plane, 0)
        near_up = send(rbuf.at[:, depth + 1], rbuf.at[:, 1], r_send.at[1], r_recv.at[1], above)
        lax.fori_loop(depth - 2, depth - 1, residual_plane, 0)
        narrowed(rbuf.at[:, depth], far_out.at[1])
        far_up = send(far_out.at[1], far_in.at[1], g_send.at[1], g_recv.at[1], above)
        shared(1)

    with jax.named_scope("image"):
        lax.fori_loop(2, depth - 2, image_plane, 0)
        share_rows(2, qbuf, peer_q, 0, 0)
        near_up.wait_recv()
        far_up.wait_recv()
        widened(far_in.at[1], rbuf.at[:, 0])
        lax.fori_loop(0, 2, image_plane, 0)
        narrowed(qbuf.at[:, 0:2, 0:half], edge_out.at[0])
        q_down = send(edge_out.at[0], edge_in.at[0], q_send.at[0], q_recv.at[0], below)
        near_down.wait_recv()
        far_down.wait_recv()
        widened(far_in.at[0], rbuf.at[:, depth + 3])
        lax.fori_loop(depth - 2, depth, image_plane, 0)
        narrowed(qbuf.at[:, depth - 2 : depth, half:width], edge_out.at[1])
        q_up = send(edge_out.at[1], edge_in.at[1], q_send.at[1], q_recv.at[1], above)
        share_rows(2, qbuf, peer_q, 0, 1)

    with jax.named_scope("energy"):
        lax.fori_loop(0, depth - 2, energy_plane, 0)
        q_down.wait_recv()
        widened(edge_in.at[0], qbuf.at[:, depth : depth + 2, 0:half])
        lax.fori_loop(depth - 2, depth, energy_plane, 0)
        q_up.wait_recv()

        def crossing(i, totals):
            start = i * CHUNK
            mine = pl.ds(pl.multiple_of(half + start, CHUNK), CHUNK)
            theirs = pl.ds(pl.multiple_of(start, CHUNK), CHUNK)
            near = [edge_in[1, part, 1, theirs, :].astype(jnp.float32) for part in range(2)]
            far = [edge_in[1, part, 0, theirs, :].astype(jnp.float32) for part in range(2)]
            zeroth = [qbuf[part, 0, mine, :] for part in range(2)]
            first = [qbuf[part, 1, mine, :] for part in range(2)]
            one = cmul(zeroth, [32.0 * near[part] - 2.0 * far[part] for part in range(2)])
            two = cmul(first, near)
            return tuple(
                totals[part] + fold((one[part] - 2.0 * two[part]) * (1.0 / 24.0)) for part in range(2)
            )

        zero = jnp.zeros((8, length), jnp.float32)
        totals = lax.fori_loop(0, half // CHUNK, crossing, (zero, zero))
        acc[12] += totals[0]
        acc[13] += totals[1]

    with jax.named_scope("scalars"):
        partial = jnp.sum(acc[...], axis=1)
        lanes = partial[:, 0:128]
        for at in range(128, length, 128):
            lanes = lanes + partial[:, at : at + 128]
        sums[0] = lanes
        scalar_copies = [
            send(
                sums.at[0],
                sums.at[k],
                s_send.at[k],
                s_recv.at[k],
                (node, lax.rem(slab + k, slabs)),
            )
            for k in range(1, slabs)
        ]
        for copy in scalar_copies:
            copy.wait_recv()
        total = jnp.zeros((SUMS, 128), jnp.float32)
        for owner in range(slabs):
            total = total + sums[lax.rem(slab - owner + slabs, slabs)]
        total = jnp.broadcast_to(jnp.sum(total, axis=1, keepdims=True), (SUMS, length))
        pair = lambda i: (total[i : i + 1], total[i + 1 : i + 2])
        s0, t0, t1, s1, s2, t2, s3 = (pair(i) for i in range(0, 14, 2))
        step0 = cdiv(s0, s1)
        square = cmul(step0, step0)
        norm1 = cmul(square, s2)
        norm1 = norm1[0] - s0[0], norm1[1] - s0[1]
        ratio = cdiv(norm1, s0)
        grow = ratio[0] + 1.0, ratio[1]
        one = cmul(cmul(grow, grow), s1)
        two = cmul(cmul(grow, step0), s2)
        three = cmul(square, s3)
        step1 = cdiv(
            norm1, (one[0] - 2.0 * two[0] + three[0], one[1] - 2.0 * two[1] + three[1])
        )
        coef_r = cmul(step1, grow)
        coef_r = coef_r[0] + step0[0], coef_r[1] + step0[1]
        coef_q = cmul(step1, step0)
        coef_q = -coef_q[0], -coef_q[1]
        inner_r, inner_q = cmul(coef_r, t1), cmul(coef_q, t2)
        inner = t0[0] + inner_r[0] + inner_q[0], t0[1] + inner_r[1] + inner_q[1]
        weight = weight_ref[0, 0], weight_ref[0, 1]
        share = cmul(weight, inner)
        following = cmul(weight, ((shift[0] - 4.0) * 0.2, shift[1] * 0.2))
        row = lax.broadcasted_iota(jnp.int32, (16, 128), 0)
        note = jnp.zeros((16, 128), jnp.float32)
        entries = (*weight, *following, *(v[:, 0:128] for v in (*share, *coef_r, *coef_q)))
        for i, entry in enumerate(entries):
            note = jnp.where(row == i, entry, note)
        notes[0] = note
        note_copies = [
            send(notes.at[0], notes.at[k], n_send.at[k], n_recv.at[k], (lax.rem(node + k, nodes), slab))
            for k in range(1, nodes)
        ]

    with jax.named_scope("moments"):
        late_first = depth - 2
        late_copies = []

        def late_plane(p):
            def step(i, carry):
                rows = pl.ds(pl.multiple_of(i * CHUNK, CHUNK), CHUNK)
                r = rbuf[0, p + 2, rows, :], rbuf[1, p + 2, rows, :]
                q = qbuf[0, p, rows, :], qbuf[1, p, rows, :]
                along_r, along_q = cmul(coef_r, r), cmul(coef_q, q)
                for part in range(2):
                    start = xbuf[part, p + 2, rows, :].astype(jnp.float32)
                    late[p - late_first, part, rows, :] = start + along_r[part] + along_q[part]
                return carry

            lax.fori_loop(0, width // CHUNK, step, 0)

        for p in range(late_first, depth):
            late_plane(p)
            for k in range(1, nodes):
                peer = lax.rem(node + k, nodes)
                late_copies.append(
                    send(
                        late.at[p - late_first, :, pl.ds(pl.multiple_of(peer * block, 8), block), :],
                        peer_late.at[k, p - late_first],
                        e_send.at[k, 6 + p - late_first],
                        e_recv.at[k, 6 + p - late_first],
                        (peer, slab),
                    )
                )

        for copy in note_copies:
            copy.wait_recv()
        whole_trace = jnp.zeros((16, 128), jnp.float32)
        for owner in range(nodes):
            whole_trace = whole_trace + notes[lax.rem(node - owner + nodes, nodes)]
        lane = lax.broadcasted_iota(jnp.int32, (16, 128), 1)
        for part in range(2):
            trace[part] = jnp.sum(jnp.where((row == 4 + part) & (lane == 0), whole_trace, 0.0))
        factors = []
        for k in range(nodes):
            first_lane = jnp.where(lane == 0, notes[k], 0.0)
            wide = jnp.broadcast_to(jnp.sum(first_lane, axis=1, keepdims=True), (16, length))
            factors.append([(wide[i : i + 1], wide[i + 1 : i + 2]) for i in (0, 2, 6, 8)])
        piece = 16 if narrow else 8

        def late_moment_plane(at, carry):
            def step(i, inner_carry):
                there = pl.ds(pl.multiple_of(i * piece, piece), piece)
                here = pl.ds(pl.multiple_of(node * block + i * piece, piece), piece)
                values = [None] * 4
                for k in range(nodes):
                    if k:
                        field = [peer_late[k, at, part, there, :] for part in range(2)]
                    else:
                        field = [late[at, part, here, :] for part in range(2)]
                    for degree in range(2):
                        term = cmul(factors[k][degree], field)
                        for part in range(2):
                            n = 2 * degree + part
                            values[n] = term[part] if k == 0 else values[n] + term[part]
                for degree in range(2):
                    for part in range(2):
                        moments[degree, 0, part, late_first + at, there, :] = values[2 * degree + part]
                return inner_carry

            lax.fori_loop(0, block // piece, step, 0)
            return carry

        def moment_plane(p, carry):
            def step(i, inner_carry):
                there = pl.ds(pl.multiple_of(i * piece, piece), piece)
                here = pl.ds(pl.multiple_of(node * block + i * piece, piece), piece)
                values = [None] * 4
                for k in range(nodes):
                    if k:
                        x, r, q = (
                            [ref[k, part, p, there, :] for part in range(2)]
                            for ref in (peer_x, peer_r, peer_q)
                        )
                    else:
                        if narrow:
                            x = [xbuf[part, p + 2, here, :] for part in range(2)]
                        else:
                            x = [xwide[part, p, here, :] for part in range(2)]
                        r = [rbuf[part, p + 2, here, :] for part in range(2)]
                        q = [qbuf[part, p, here, :] for part in range(2)]
                    along_r, along_q = cmul(factors[k][2], r), cmul(factors[k][3], q)
                    field = [
                        x[part].astype(jnp.float32) + along_r[part] + along_q[part]
                        for part in range(2)
                    ]
                    for degree in range(2):
                        term = cmul(factors[k][degree], field)
                        for part in range(2):
                            at = 2 * degree + part
                            values[at] = term[part] if k == 0 else values[at] + term[part]
                for degree in range(2):
                    for part in range(2):
                        moments[degree, 0, part, p, there, :] = values[2 * degree + part]
                return inner_carry

            lax.fori_loop(0, block // piece, step, 0)
            return carry

        for group, (first, last) in enumerate(groups[:2]):
            for kind in range(3):
                for copy in early[kind, group]:
                    copy.wait_recv()
            lax.fori_loop(first, last, moment_plane, 0)

        for at in range(2):
            for copy in late_copies[at * (nodes - 1) : (at + 1) * (nodes - 1)]:
                copy.wait_recv()
            late_moment_plane(at, 0)

    early_copies = late_copies + [copy for copies in early.values() for copy in copies]
    for copy in [x_down, x_up, near_down, near_up, far_down, far_up, q_down, q_up]:
        copy.wait_send()
    for copy in [*scalar_copies, *note_copies, *early_copies]:
        copy.wait_send()


def per_device(nodes, slabs, probes, potential, warm_start, shift_points, quad_weights):
    depth, width, length = potential.shape
    block = width // nodes
    narrow = block % 16 == 0
    f32, bf16 = jnp.float32, jnp.bfloat16
    anywhere = pl.BlockSpec(memory_space=pltpu.HBM)
    scalars = pl.BlockSpec(memory_space=pltpu.SMEM)
    vector = pl.BlockSpec(memory_space=pltpu.VMEM)
    dma = pltpu.SemaphoreType.DMA
    return pl.pallas_call(
        functools.partial(kernel, nodes, slabs),
        out_shape=(
            jax.ShapeDtypeStruct((2, 1, 2, depth, block, length), f32),
            jax.ShapeDtypeStruct((2,), f32),
        ),
        in_specs=[anywhere] * 7,
        out_specs=(vector, scalars),
        scratch_shapes=[
            pltpu.VMEM((2, depth + 4, width, length), bf16),
            pltpu.VMEM((depth, width, length), f32),
            pltpu.VMEM((depth, width, length), f32),
            pltpu.VMEM((2, depth + 4, width, length), f32),
            pltpu.VMEM((2, depth + 2, width, length), f32),
            pltpu.VMEM((2, width, length), f32),
            pltpu.VMEM((SUMS, 8, length), f32),
            pltpu.VMEM((slabs, SUMS, 128), f32),
            pltpu.VMEM((2, 2, width, length), bf16),
            pltpu.VMEM((2, 2, width, length), bf16),
            pltpu.VMEM((2, 2, 2, width // 2, length), bf16),
            pltpu.VMEM((2, 2, 2, width // 2, length), bf16),
            pltpu.VMEM((8, 128) if narrow else (2, depth, width, length), f32),
            pltpu.VMEM((nodes, 2, depth, block, length), bf16 if narrow else f32),
            pltpu.VMEM((nodes, 2, depth, block, length), f32),
            pltpu.VMEM((nodes, 2, depth, block, length), f32),
            pltpu.VMEM((2, 2, width, length), f32),
            pltpu.VMEM((nodes, 2, 2, block, length), f32),
            pltpu.VMEM((nodes, 16, 128), f32),
            pltpu.SMEM((1, 2), f32),
            pltpu.SMEM((1, 2), f32),
            pltpu.VMEM((width, width), bf16),
            pltpu.VMEM((length, length), bf16),
            dma((7,)),
            dma((2,)),
            dma((2,)),
            dma((2,)),
            dma((2,)),
            dma((2,)),
            dma((2,)),
            dma((slabs,)),
            dma((slabs,)),
            dma((nodes,)),
            dma((nodes,)),
            dma((2,)),
            dma((2,)),
            dma((nodes, 8)),
            dma((nodes, 8)),
        ],
        compiler_params=pltpu.CompilerParams(
            collective_id=0, has_side_effects=True, vmem_limit_bytes=64 * 1024 * 1024
        ),
    )(
        warm_start,
        probes,
        potential,
        shift_points,
        quad_weights,
        jnp.asarray(ring_matrix(width, 0.0)),
        jnp.asarray(ring_matrix(length, -90.0)),
    )


def solution(mesh):
    return jax.shard_map(
        functools.partial(per_device, mesh.shape["node"], mesh.shape["grid"]),
        mesh=mesh,
        in_specs=(
            P(None, "grid", None, None),
            P("grid", None, None),
            P("node", None, None, "grid", None, None),
            P("node", None),
            P("node", None),
        ),
        out_specs=(P(None, None, None, "grid", "node", None), P()),
        check_vma=False,
    )
```

```python
import functools

import jax
import jax.numpy as jnp
import ml_dtypes
import numpy as np
from jax import lax
from jax.experimental import pallas as pl
from jax.experimental.pallas import tpu as pltpu
from jax.sharding import PartitionSpec as P

MESH = pl.DeviceIdType.MESH
SUMS = 16
CHUNK = 32


def ring_matrix(size, diagonal):
    matrix = np.zeros((size, size), np.float32)
    at = np.arange(size)
    for step, weight in ((1, 16.0), (2, -1.0)):
        matrix[at, (at + step) % size] += weight
        matrix[at, (at - step) % size] += weight
    matrix[at, at] += diagonal
    return matrix.astype(ml_dtypes.bfloat16)


def cmul(a, b):
    return a[0] * b[0] - a[1] * b[1], a[0] * b[1] + a[1] * b[0]


def cdiv(a, b):
    size = b[0] * b[0] + b[1] * b[1]
    return (a[0] * b[0] + a[1] * b[1]) / size, (a[1] * b[0] - a[0] * b[1]) / size


def fold(values):
    rows, cols = values.shape
    return jnp.sum(values.reshape(rows // 8, 8, cols), axis=0)


def kernel(
    nodes,
    slabs,
    warm,
    probes,
    potential,
    shift_hbm,
    weight_hbm,
    along_x_hbm,
    along_y_hbm,
    moments,
    trace,
    xbuf,
    bbuf,
    vbuf,
    rbuf,
    qbuf,
    plane,
    acc,
    sums,
    far_out,
    far_in,
    edge_out,
    edge_in,
    xwide,
    peer_x,
    peer_r,
    peer_q,
    late,
    peer_late,
    notes,
    shift_ref,
    weight_ref,
    along_x,
    along_y,
    local_sem,
    x_send,
    x_recv,
    r_send,
    r_recv,
    q_send,
    q_recv,
    s_send,
    s_recv,
    n_send,
    n_recv,
    g_send,
    g_recv,
    e_send,
    e_recv,
):
    node, slab = lax.axis_index("node"), lax.axis_index("grid")
    depth, width, length = bbuf.shape
    half = width // 2
    block = width // nodes
    above = (node, lax.rem(slab + 1, slabs))
    below = (node, lax.rem(slab + slabs - 1, slabs))

    loads = [
        pltpu.make_async_copy(warm.at[0, 0], xbuf.at[:, 2 : depth + 2], local_sem.at[0]),
        pltpu.make_async_copy(probes.at[0], bbuf, local_sem.at[1]),
        pltpu.make_async_copy(potential, vbuf, local_sem.at[2]),
        pltpu.make_async_copy(shift_hbm, shift_ref, local_sem.at[3]),
        pltpu.make_async_copy(weight_hbm, weight_ref, local_sem.at[4]),
        pltpu.make_async_copy(along_x_hbm, along_x, local_sem.at[5]),
        pltpu.make_async_copy(along_y_hbm, along_y, local_sem.at[6]),
    ]
    for load in loads:
        load.start()

    barrier = pltpu.get_barrier_semaphore()
    for k in range(1, slabs):
        pl.semaphore_signal(
            barrier, inc=1, device_id=(node, lax.rem(slab + k, slabs)), device_id_type=MESH
        )
    for k in range(1, nodes):
        pl.semaphore_signal(
            barrier, inc=1, device_id=(lax.rem(node + k, nodes), slab), device_id_type=MESH
        )
    pl.semaphore_wait(barrier, slabs + nodes - 2)

    def send(source, target, send_sem, recv_sem, device):
        copy = pltpu.make_async_remote_copy(
            src_ref=source,
            dst_ref=target,
            send_sem=send_sem,
            recv_sem=recv_sem,
            device_id=device,
            device_id_type=MESH,
        )
        copy.start()
        return copy

    x_down = send(
        warm.at[0, 0, :, 0:2], xbuf.at[:, depth + 2 : depth + 4], x_send.at[0], x_recv.at[0], below
    )
    x_up = send(warm.at[0, 0, :, depth - 2 : depth], xbuf.at[:, 0:2], x_send.at[1], x_recv.at[1], above)

    groups = ((2, depth - 3), (0, 2))
    early = {}

    def share_rows(kind, source, target, offset, group):
        first, last = groups[group]
        slot = 2 * kind + group
        step = 16 if block % 16 == 0 else 8
        copies = []
        for k in range(1, nodes):
            peer = lax.rem(node + k, nodes)
            rows = pl.ds(pl.multiple_of(peer * block, step), block)
            copies.append(
                send(
                    source.at[:, first + offset : last + offset, rows, :],
                    target.at[k, :, first:last],
                    e_send.at[k, slot],
                    e_recv.at[k, slot],
                    (peer, slab),
                )
            )
        early[kind, group] = copies

    narrow = block % 16 == 0
    if narrow:
        for group in range(2):
            share_rows(0, warm.at[0, 0], peer_x, 0, group)

    acc[...] = jnp.zeros_like(acc)
    qbuf[:, depth : depth + 2, half:, :] = jnp.zeros((2, 2, width - half, length), jnp.float32)
    for load in loads:
        load.wait()
    shift = shift_ref[0, 0], shift_ref[0, 1]

    def dot(a, b):
        return jnp.dot(a, b, preferred_element_type=jnp.float32)

    def in_plane_exact(p):
        for part in range(2):
            field = xbuf[part, p + 2]
            plane[part] = dot(field, along_y[...]) + dot(along_x[...], field)

    def in_plane(source, p):
        for part in range(2):
            field = source[part, p]
            high = field.astype(jnp.bfloat16)
            low = (field - high.astype(jnp.float32)).astype(jnp.bfloat16)
            plane[part] = (dot(high, along_y[...]) + dot(low, along_y[...])) + (
                dot(along_x[...], high) + dot(along_x[...], low)
            )

    def apply(field, stencil, local):
        diagonal = shift[0] - local
        return (
            diagonal * field[0] - shift[1] * field[1] + stencil[0] * (1.0 / 24.0),
            diagonal * field[1] + shift[1] * field[0] + stencil[1] * (1.0 / 24.0),
        )

    def in_chunks(first, terms):
        count = terms[1]

        def step(i, totals):
            rows = pl.ds(pl.multiple_of(i * CHUNK, CHUNK), CHUNK)
            values = terms[0](rows)
            return tuple(total + fold(value) for total, value in zip(totals, values))

        zero = jnp.zeros((8, length), jnp.float32)
        totals = lax.fori_loop(0, width // CHUNK, step, (zero,) * count)
        for i, total in enumerate(totals):
            acc[first + i] += total

    def residual_plane(p, carry):
        in_plane_exact(p)

        def terms(rows):
            stencil, field = [], []
            for part in range(2):
                at = [xbuf[part, p + j, rows, :].astype(jnp.float32) for j in range(5)]
                stencil.append(plane[part, rows, :] + 16.0 * (at[1] + at[3]) - (at[0] + at[4]))
                field.append(at[2])
            source = bbuf[p, rows, :]
            image = apply(field, stencil, vbuf[p, rows, :])
            r = source - image[0], -image[1]
            if not narrow:
                for part in range(2):
                    xwide[part, p, rows, :] = field[part]
            rbuf[0, p + 2, rows, :] = r[0]
            rbuf[1, p + 2, rows, :] = r[1]
            return (
                r[0] * r[0] - r[1] * r[1],
                2.0 * r[0] * r[1],
                source * field[0],
                source * field[1],
                source * r[0],
                source * r[1],
            )

        in_chunks(0, (terms, 6))
        return carry

    def image_plane(p, carry):
        in_plane(rbuf, p + 2)

        def terms(rows):
            stencil, field = [], []
            for part in range(2):
                at = [rbuf[part, p + j, rows, :] for j in range(5)]
                stencil.append(plane[part, rows, :] + 16.0 * (at[1] + at[3]) - (at[0] + at[4]))
                field.append(at[2])
            source = bbuf[p, rows, :]
            q = apply(field, stencil, vbuf[p, rows, :])
            qbuf[0, p, rows, :] = q[0]
            qbuf[1, p, rows, :] = q[1]
            return (
                *cmul(field, q),
                q[0] * q[0] - q[1] * q[1],
                2.0 * q[0] * q[1],
                source * q[0],
                source * q[1],
            )

        in_chunks(6, (terms, 6))
        return carry

    def energy_plane(p, carry):
        in_plane(qbuf, p)

        def terms(rows):
            stencil, field = [], []
            for part in range(2):
                stencil.append(
                    plane[part, rows, :]
                    + 32.0 * qbuf[part, p + 1, rows, :]
                    - 2.0 * qbuf[part, p + 2, rows, :]
                )
                field.append(qbuf[part, p, rows, :])
            return cmul(field, apply(field, stencil, vbuf[p, rows, :]))

        in_chunks(12, (terms, 2))
        return carry

    def narrowed(source, target):
        target[...] = source[...].astype(jnp.bfloat16)

    def widened(source, target):
        target[...] = source[...].astype(jnp.float32)

    def shared(group):
        if not narrow:
            share_rows(0, xwide, peer_x, 0, group)
        share_rows(1, rbuf, peer_r, 2, group)

    with jax.named_scope("residual"):
        lax.fori_loop(2, depth - 2, residual_plane, 0)
        shared(0)
        x_up.wait_recv()
        x_down.wait_recv()
        lax.fori_loop(0, 2, residual_plane, 0)
        near_down = send(
            rbuf.at[:, 2], rbuf.at[:, depth + 2], r_send.at[0], r_recv.at[0], below
        )
        narrowed(rbuf.at[:, 3], far_out.at[0])
        far_down = send(far_out.at[0], far_in.at[0], g_send.at[0], g_recv.at[0], below)
        lax.fori_loop(depth - 2, depth, residual_plane, 0)
        near_up = send(rbuf.at[:, depth + 1], rbuf.at[:, 1], r_send.at[1], r_recv.at[1], above)
        narrowed(rbuf.at[:, depth], far_out.at[1])
        far_up = send(far_out.at[1], far_in.at[1], g_send.at[1], g_recv.at[1], above)
        shared(1)

    with jax.named_scope("image"):
        lax.fori_loop(2, depth - 2, image_plane, 0)
        share_rows(2, qbuf, peer_q, 0, 0)
        near_up.wait_recv()
        far_up.wait_recv()
        widened(far_in.at[1], rbuf.at[:, 0])
        lax.fori_loop(0, 2, image_plane, 0)
        narrowed(qbuf.at[:, 0:2, 0:half], edge_out.at[0])
        q_down = send(edge_out.at[0], edge_in.at[0], q_send.at[0], q_recv.at[0], below)
        near_down.wait_recv()
        far_down.wait_recv()
        widened(far_in.at[0], rbuf.at[:, depth + 3])
        lax.fori_loop(depth - 2, depth, image_plane, 0)
        narrowed(qbuf.at[:, depth - 2 : depth, half:width], edge_out.at[1])
        q_up = send(edge_out.at[1], edge_in.at[1], q_send.at[1], q_recv.at[1], above)
        share_rows(2, qbuf, peer_q, 0, 1)

    with jax.named_scope("energy"):
        lax.fori_loop(0, depth - 2, energy_plane, 0)
        q_down.wait_recv()
        widened(edge_in.at[0], qbuf.at[:, depth : depth + 2, 0:half])
        lax.fori_loop(depth - 2, depth, energy_plane, 0)
        q_up.wait_recv()

        def crossing(i, totals):
            start = i * CHUNK
            mine = pl.ds(pl.multiple_of(half + start, CHUNK), CHUNK)
            theirs = pl.ds(pl.multiple_of(start, CHUNK), CHUNK)
            near = [edge_in[1, part, 1, theirs, :].astype(jnp.float32) for part in range(2)]
            far = [edge_in[1, part, 0, theirs, :].astype(jnp.float32) for part in range(2)]
            zeroth = [qbuf[part, 0, mine, :] for part in range(2)]
            first = [qbuf[part, 1, mine, :] for part in range(2)]
            one = cmul(zeroth, [32.0 * near[part] - 2.0 * far[part] for part in range(2)])
            two = cmul(first, near)
            return tuple(
                totals[part] + fold((one[part] - 2.0 * two[part]) * (1.0 / 24.0)) for part in range(2)
            )

        zero = jnp.zeros((8, length), jnp.float32)
        totals = lax.fori_loop(0, half // CHUNK, crossing, (zero, zero))
        acc[12] += totals[0]
        acc[13] += totals[1]

    with jax.named_scope("scalars"):
        partial = jnp.sum(acc[...], axis=1)
        lanes = partial[:, 0:128]
        for at in range(128, length, 128):
            lanes = lanes + partial[:, at : at + 128]
        sums[0] = lanes
        scalar_copies = [
            send(
                sums.at[0],
                sums.at[k],
                s_send.at[k],
                s_recv.at[k],
                (node, lax.rem(slab + k, slabs)),
            )
            for k in range(1, slabs)
        ]
        for copy in scalar_copies:
            copy.wait_recv()
        total = jnp.zeros((SUMS, 128), jnp.float32)
        for owner in range(slabs):
            total = total + sums[lax.rem(slab - owner + slabs, slabs)]
        total = jnp.broadcast_to(jnp.sum(total, axis=1, keepdims=True), (SUMS, length))
        pair = lambda i: (total[i : i + 1], total[i + 1 : i + 2])
        s0, t0, t1, s1, s2, t2, s3 = (pair(i) for i in range(0, 14, 2))
        step0 = cdiv(s0, s1)
        square = cmul(step0, step0)
        norm1 = cmul(square, s2)
        norm1 = norm1[0] - s0[0], norm1[1] - s0[1]
        ratio = cdiv(norm1, s0)
        grow = ratio[0] + 1.0, ratio[1]
        one = cmul(cmul(grow, grow), s1)
        two = cmul(cmul(grow, step0), s2)
        three = cmul(square, s3)
        step1 = cdiv(
            norm1, (one[0] - 2.0 * two[0] + three[0], one[1] - 2.0 * two[1] + three[1])
        )
        coef_r = cmul(step1, grow)
        coef_r = coef_r[0] + step0[0], coef_r[1] + step0[1]
        coef_q = cmul(step1, step0)
        coef_q = -coef_q[0], -coef_q[1]
        inner_r, inner_q = cmul(coef_r, t1), cmul(coef_q, t2)
        inner = t0[0] + inner_r[0] + inner_q[0], t0[1] + inner_r[1] + inner_q[1]
        weight = weight_ref[0, 0], weight_ref[0, 1]
        share = cmul(weight, inner)
        following = cmul(weight, ((shift[0] - 4.0) * 0.2, shift[1] * 0.2))
        row = lax.broadcasted_iota(jnp.int32, (16, 128), 0)
        note = jnp.zeros((16, 128), jnp.float32)
        entries = (*weight, *following, *(v[:, 0:128] for v in (*share, *coef_r, *coef_q)))
        for i, entry in enumerate(entries):
            note = jnp.where(row == i, entry, note)
        notes[0] = note
        note_copies = [
            send(notes.at[0], notes.at[k], n_send.at[k], n_recv.at[k], (lax.rem(node + k, nodes), slab))
            for k in range(1, nodes)
        ]

    with jax.named_scope("moments"):
        late_first = depth - 3
        late_copies = []

        def late_plane(p):
            def step(i, carry):
                rows = pl.ds(pl.multiple_of(i * CHUNK, CHUNK), CHUNK)
                r = rbuf[0, p + 2, rows, :], rbuf[1, p + 2, rows, :]
                q = qbuf[0, p, rows, :], qbuf[1, p, rows, :]
                along_r, along_q = cmul(coef_r, r), cmul(coef_q, q)
                for part in range(2):
                    start = xbuf[part, p + 2, rows, :].astype(jnp.float32)
                    late[p - late_first, part, rows, :] = start + along_r[part] + along_q[part]
                return carry

            lax.fori_loop(0, width // CHUNK, step, 0)

        for p in range(late_first, depth):
            late_plane(p)
            for k in range(1, nodes):
                peer = lax.rem(node + k, nodes)
                late_copies.append(
                    send(
                        late.at[p - late_first, :, pl.ds(pl.multiple_of(peer * block, 8), block), :],
                        peer_late.at[k, p - late_first],
                        e_send.at[k, 6 + p - late_first],
                        e_recv.at[k, 6 + p - late_first],
                        (peer, slab),
                    )
                )

        for copy in note_copies:
            copy.wait_recv()
        whole_trace = jnp.zeros((16, 128), jnp.float32)
        for owner in range(nodes):
            whole_trace = whole_trace + notes[lax.rem(node - owner + nodes, nodes)]
        lane = lax.broadcasted_iota(jnp.int32, (16, 128), 1)
        for part in range(2):
            trace[part] = jnp.sum(jnp.where((row == 4 + part) & (lane == 0), whole_trace, 0.0))
        factors = []
        for k in range(nodes):
            first_lane = jnp.where(lane == 0, notes[k], 0.0)
            wide = jnp.broadcast_to(jnp.sum(first_lane, axis=1, keepdims=True), (16, length))
            factors.append([(wide[i : i + 1], wide[i + 1 : i + 2]) for i in (0, 2, 6, 8)])
        piece = 16 if narrow else 8

        def late_moment_plane(at, carry):
            def step(i, inner_carry):
                there = pl.ds(pl.multiple_of(i * piece, piece), piece)
                here = pl.ds(pl.multiple_of(node * block + i * piece, piece), piece)
                values = [None] * 4
                for k in range(nodes):
                    if k:
                        field = [peer_late[k, at, part, there, :] for part in range(2)]
                    else:
                        field = [late[at, part, here, :] for part in range(2)]
                    for degree in range(2):
                        term = cmul(factors[k][degree], field)
                        for part in range(2):
                            n = 2 * degree + part
                            values[n] = term[part] if k == 0 else values[n] + term[part]
                for degree in range(2):
                    for part in range(2):
                        moments[degree, 0, part, late_first + at, there, :] = values[2 * degree + part]
                return inner_carry

            lax.fori_loop(0, block // piece, step, 0)
            return carry

        def moment_plane(p, carry):
            def step(i, inner_carry):
                there = pl.ds(pl.multiple_of(i * piece, piece), piece)
                here = pl.ds(pl.multiple_of(node * block + i * piece, piece), piece)
                values = [None] * 4
                for k in range(nodes):
                    if k:
                        x, r, q = (
                            [ref[k, part, p, there, :] for part in range(2)]
                            for ref in (peer_x, peer_r, peer_q)
                        )
                    else:
                        if narrow:
                            x = [xbuf[part, p + 2, here, :] for part in range(2)]
                        else:
                            x = [xwide[part, p, here, :] for part in range(2)]
                        r = [rbuf[part, p + 2, here, :] for part in range(2)]
                        q = [qbuf[part, p, here, :] for part in range(2)]
                    along_r, along_q = cmul(factors[k][2], r), cmul(factors[k][3], q)
                    field = [
                        x[part].astype(jnp.float32) + along_r[part] + along_q[part]
                        for part in range(2)
                    ]
                    for degree in range(2):
                        term = cmul(factors[k][degree], field)
                        for part in range(2):
                            at = 2 * degree + part
                            values[at] = term[part] if k == 0 else values[at] + term[part]
                for degree in range(2):
                    for part in range(2):
                        moments[degree, 0, part, p, there, :] = values[2 * degree + part]
                return inner_carry

            lax.fori_loop(0, block // piece, step, 0)
            return carry

        for group, (first, last) in enumerate(groups):
            for kind in range(3):
                for copy in early[kind, group]:
                    copy.wait_recv()
            lax.fori_loop(first, last, moment_plane, 0)

        for at in range(3):
            for copy in late_copies[at * (nodes - 1) : (at + 1) * (nodes - 1)]:
                copy.wait_recv()
            late_moment_plane(at, 0)

    early_copies = late_copies + [copy for copies in early.values() for copy in copies]
    for copy in [x_down, x_up, near_down, near_up, far_down, far_up, q_down, q_up]:
        copy.wait_send()
    for copy in [*scalar_copies, *note_copies, *early_copies]:
        copy.wait_send()


def per_device(nodes, slabs, probes, potential, warm_start, shift_points, quad_weights):
    depth, width, length = potential.shape
    block = width // nodes
    narrow = block % 16 == 0
    f32, bf16 = jnp.float32, jnp.bfloat16
    anywhere = pl.BlockSpec(memory_space=pltpu.HBM)
    scalars = pl.BlockSpec(memory_space=pltpu.SMEM)
    vector = pl.BlockSpec(memory_space=pltpu.VMEM)
    dma = pltpu.SemaphoreType.DMA
    return pl.pallas_call(
        functools.partial(kernel, nodes, slabs),
        out_shape=(
            jax.ShapeDtypeStruct((2, 1, 2, depth, block, length), f32),
            jax.ShapeDtypeStruct((2,), f32),
        ),
        in_specs=[anywhere] * 7,
        out_specs=(vector, scalars),
        scratch_shapes=[
            pltpu.VMEM((2, depth + 4, width, length), bf16),
            pltpu.VMEM((depth, width, length), f32),
            pltpu.VMEM((depth, width, length), f32),
            pltpu.VMEM((2, depth + 4, width, length), f32),
            pltpu.VMEM((2, depth + 2, width, length), f32),
            pltpu.VMEM((2, width, length), f32),
            pltpu.VMEM((SUMS, 8, length), f32),
            pltpu.VMEM((slabs, SUMS, 128), f32),
            pltpu.VMEM((2, 2, width, length), bf16),
            pltpu.VMEM((2, 2, width, length), bf16),
            pltpu.VMEM((2, 2, 2, width // 2, length), bf16),
            pltpu.VMEM((2, 2, 2, width // 2, length), bf16),
            pltpu.VMEM((8, 128) if narrow else (2, depth, width, length), f32),
            pltpu.VMEM((nodes, 2, depth, block, length), bf16 if narrow else f32),
            pltpu.VMEM((nodes, 2, depth, block, length), f32),
            pltpu.VMEM((nodes, 2, depth, block, length), f32),
            pltpu.VMEM((3, 2, width, length), f32),
            pltpu.VMEM((nodes, 3, 2, block, length), f32),
            pltpu.VMEM((nodes, 16, 128), f32),
            pltpu.SMEM((1, 2), f32),
            pltpu.SMEM((1, 2), f32),
            pltpu.VMEM((width, width), bf16),
            pltpu.VMEM((length, length), bf16),
            dma((7,)),
            dma((2,)),
            dma((2,)),
            dma((2,)),
            dma((2,)),
            dma((2,)),
            dma((2,)),
            dma((slabs,)),
            dma((slabs,)),
            dma((nodes,)),
            dma((nodes,)),
            dma((2,)),
            dma((2,)),
            dma((nodes, 9)),
            dma((nodes, 9)),
        ],
        compiler_params=pltpu.CompilerParams(
            collective_id=0, has_side_effects=True, vmem_limit_bytes=64 * 1024 * 1024
        ),
    )(
        warm_start,
        probes,
        potential,
        shift_points,
        quad_weights,
        jnp.asarray(ring_matrix(width, 0.0)),
        jnp.asarray(ring_matrix(length, -90.0)),
    )


def solution(mesh):
    return jax.shard_map(
        functools.partial(per_device, mesh.shape["node"], mesh.shape["grid"]),
        mesh=mesh,
        in_specs=(
            P(None, "grid", None, None),
            P("grid", None, None),
            P("node", None, None, "grid", None, None),
            P("node", None),
            P("node", None),
        ),
        out_specs=(P(None, None, None, "grid", "node", None), P()),
        check_vma=False,
    )
```
